32 devices in a mesh: dp: 8 (over z, y), tp: 4 (over x, core).
Axes of the slice: x: 2, y: 2, z: 4, core: 2. Of those that a mesh axis runs over, the one named last changes fastest.
Arguments:
- inputs: bfloat16 [32, 896, 512], P('dp', 'tp'), may hold values from -6 to 6
- dataset: int32 [32], P('dp'), may hold values from 0 to 3, as said below
- variate_mask: int32 [32, 896], P('dp'), may hold values from 0 to 1, as said below
- dataset_bias: bfloat16 [4, 512], replicated, may hold values from -3 to 3
- w_qkv: bfloat16 [3, 512, 512], P(None, None, 'tp'), may hold values from -0.25 to 0.25
- qv_bias: bfloat16 [2, 512], P(None, 'tp'), may hold values from -1.796875 to 1.796875
- w_out: bfloat16 [512, 512], P('tp'), may hold values from -1 to 1
- out_bias: bfloat16 [2, 512], replicated, may hold values from -1.796875 to 1.796875
- w_up: bfloat16 [512, 2048], P(None, 'tp'), may hold values from -0.25 to 0.25
- up_bias: bfloat16 [2048], P('tp'), may hold values from -1.796875 to 1.796875
- w_down: bfloat16 [2048, 512], P('tp'), may hold values from -0.125 to 0.125
- norm_gain: bfloat16 [2, 512], replicated, may hold values from 0.25 to 1.75
- norm_shift: bfloat16 [2, 512], replicated, may hold values from -1.796875 to 1.796875
- cotangent: bfloat16 [32, 896, 512], P('dp', 'tp'), may hold values from -6 to 6
Outputs:
- outputs: bfloat16 [32, 896, 512], P('dp', 'tp')
- input_grad: bfloat16 [32, 896, 512], P('dp', 'tp')
- dataset_bias_grad: float32 [4, 512], replicated
- w_qkv_grad: float32 [3, 512, 512], P(None, None, 'tp')
- qv_bias_grad: float32 [2, 512], P(None, 'tp')
- w_out_grad: float32 [512, 512], P('tp')
- out_bias_grad: float32 [2, 512], replicated
- w_up_grad: float32 [512, 2048], P(None, 'tp')
- up_bias_grad: float32 [2048], P('tp')
- w_down_grad: float32 [2048, 512], P('tp')
- norm_gain_grad: float32 [2, 512], replicated
- norm_shift_grad: float32 [2, 512], replicated
The draws below stay inside these ranges and needn't reach their ends.
Inputs may be any that keep to these rules, and one draw needn't show every extreme that they name: In every aligned block of 4 windows (those of one index of dp) at least one window has dataset 3. `variate_mask`: variate 0 of every window is live. A window of dataset c has no live variate at or past entry c of (max(1, 7), max(1, 21), max(1, 321), max(1, 862)).
All inputs are finite; a program needn't handle non-finite values.
Results may differ from the reference program's by a relative error of at most 0.017.
Values may be sent and summed in bfloat16 or wider, within the bound.
A program may use at most 128 MiB of HBM per device.

```python
import functools
import math
import jax
import jax.numpy as jnp
from jax import lax

D = 512
H = 8
FF = 2048
HD = 64
V = 896
DATASETS = 4
W_DEV = 4
WINDOWS = 32


def shared_draw(key):
    base_key = jax.random.fold_in(key, 11)
    first_key, second_key, third_key = jax.random.split(base_key, 3)
    dataset_ids = jax.random.randint(first_key, (WINDOWS,), 0, 4)
    picked = jax.random.randint(second_key, (WINDOWS // W_DEV,), 0, W_DEV)
    window_index = jnp.arange(WINDOWS)
    forced = window_index % W_DEV == picked[window_index // W_DEV]
    dataset_ids = jnp.where(forced, 3, dataset_ids)
    limits = jnp.array([max(1, 7 * V // 896), max(1, 21 * V // 896), max(1, 321 * V // 896), max(1, 862 * V // 896)], dtype=jnp.int32)
    counts_live = jnp.sum(jnp.where(dataset_ids[:, None] == jnp.arange(4)[None, :], limits[None, :], 0), axis=1)
    position = jnp.arange(V)
    dropped = jax.random.randint(third_key, (WINDOWS, V), 0, 16) == 0
    live_mask = (position[None, :] < counts_live[:, None]) & (~dropped | (position[None, :] == 0))
    return (dataset_ids.astype(jnp.int32), live_mask.astype(jnp.int32))


def draw_dataset(key, part):
    return shared_draw(key)[0]


def draw_variate_mask(key, part):
    return shared_draw(key)[1]


def level_of(stream_key, extent, cuts, least, top_value):
    def one(dim, shards_of):
        draws = jax.random.uniform(jax.random.fold_in(jax.random.fold_in(stream_key, 6), dim), (shards_of,), jnp.float32, least / len(cuts), top_value / len(cuts))
        return jnp.repeat(jnp.exp(draws), extent[dim] // shards_of).reshape((-1,) + (1,) * (len(extent) - dim - 1))

    factor_of = one(*cuts[0])
    for cut in cuts[1:]:
        factor_of = factor_of * one(*cut)
    return factor_of


def normal_values(rng, shape, scale, reach, pieces=(), kind=jnp.bfloat16):
    loudness = level_of(rng, shape, pieces, -0.22, 0.18) if pieces else 1.0
    result = jax.random.normal(rng, shape, jnp.float32) * scale * loudness
    return jnp.minimum(jnp.maximum(result, -reach), reach).astype(kind)


def setup_inputs(seed: int = 0) -> dict:
    arg_keys = jax.random.split(jax.random.key(seed), 15)
    inputs = normal_values(arg_keys[0], (WINDOWS, V, D), 1.0, 6.0, ((0, 8), (1, 4)))
    dataset = draw_dataset(jax.random.fold_in(arg_keys[14], 71), 0)
    variate_mask = draw_variate_mask(jax.random.fold_in(arg_keys[14], 71), 0)
    dataset_bias = normal_values(arg_keys[3], (DATASETS, D), 0.5, 3.0)
    w_qkv = normal_values(arg_keys[4], (3, D, D), D ** -0.5, 0.25, ((2, 4),))
    qv_bias = normal_values(arg_keys[5], (2, D), 0.3, 1.796875, ((1, 4),))
    w_out = normal_values(arg_keys[6], (D, D), (D // 16) ** -0.5, 1.0, ((0, 4),))
    out_bias = normal_values(arg_keys[7], (2, D), 0.3, 1.796875)
    w_up = normal_values(arg_keys[8], (D, FF), D ** -0.5, 0.25, ((1, 4),))
    up_bias = normal_values(arg_keys[9], (FF,), 0.3, 1.796875, ((0, 4),))
    w_down = normal_values(arg_keys[10], (FF, D), FF ** -0.5, 0.125, ((0, 4),))
    norm_gain = jnp.clip(1.0 + 0.15 * jax.random.normal(arg_keys[11], (2, D), jnp.float32), 0.25, 1.75).astype(jnp.bfloat16)
    norm_shift = normal_values(arg_keys[12], (2, D), 0.3, 1.796875)
    cotangent = normal_values(arg_keys[13], (WINDOWS, V, D), 1.0, 6.0, ((0, 8), (1, 4)))
    return dict(inputs=inputs, dataset=dataset, variate_mask=variate_mask, dataset_bias=dataset_bias, w_qkv=w_qkv, qv_bias=qv_bias, w_out=w_out, out_bias=out_bias, w_up=w_up, up_bias=up_bias, w_down=w_down, norm_gain=norm_gain, norm_shift=norm_shift, cotangent=cotangent)


@jax.custom_vjp
def low(v):
    return lax.optimization_barrier(v.astype(jnp.bfloat16)).astype(jnp.float32)

@jax.custom_vjp
def low_back(v):
    return v

def low_keep(v):
    return (low(v), None)

def low_pass(kept, grad):
    return (grad,)

def back_keep(v):
    return (v, None)

def back_low(kept, grad):
    return (low(grad),)
low.defvjp(low_keep, low_pass)
low_back.defvjp(back_keep, back_low)
EPSILON = 1e-05
HIGHEST = lax.Precision.HIGHEST
NEG_FILL = -1e+30

def norm_rows(residual, gains, shifts):
    center = residual - lax.optimization_barrier(jnp.mean(residual, axis=-1, keepdims=True))
    spread = lax.optimization_barrier(jnp.mean(center * center, axis=-1, keepdims=True))
    return center * lax.rsqrt(spread + EPSILON) * gains + shifts

def window_block(params, packed):
    dataset_bias, w_qkv, qv_bias, w_out, out_bias, w_up, up_bias, w_down, norm_gain, norm_shift = params
    x_rows, one_hot, live_rows = packed
    groups_here = x_rows.shape[0]
    base_rows = x_rows + jnp.dot(one_hot, dataset_bias, precision=HIGHEST)[:, None, :]
    act_in = low(base_rows)
    queries = low_back(low(jnp.einsum('gvd,de->gve', act_in, w_qkv[0], precision=HIGHEST) + qv_bias[0]))
    key_rows = low_back(low(jnp.einsum('gvd,de->gve', act_in, w_qkv[1], precision=HIGHEST)))
    value_rows = low_back(low(jnp.einsum('gvd,de->gve', act_in, w_qkv[2], precision=HIGHEST) + qv_bias[1]))
    q_heads = queries.reshape(groups_here, V, H, HD)
    k_heads = key_rows.reshape(groups_here, V, H, HD)
    v_heads = value_rows.reshape(groups_here, V, H, HD)
    scores = low_back(jnp.einsum('gqhe,gkhe->ghqk', q_heads, k_heads, precision=HIGHEST) * (1.0 / math.sqrt(HD)))
    scores = jnp.where(live_rows[:, None, None, :] > 0.5, scores, NEG_FILL)
    row_top = lax.optimization_barrier(jnp.max(scores, axis=-1, keepdims=True))
    exponent = jnp.exp(scores - row_top)
    attn_prob = low(exponent / lax.optimization_barrier(jnp.sum(exponent, axis=-1, keepdims=True)))
    mixture = jnp.einsum('ghqk,gkhe->gqhe', attn_prob, v_heads, precision=HIGHEST).reshape(groups_here, V, D)
    mixture = low_back(low(mixture))
    attended = low_back(jnp.einsum('gvh,hd->gvd', mixture, w_out, precision=HIGHEST)) + out_bias[0]
    hidden = norm_rows(base_rows + attended, norm_gain[0], norm_shift[0])
    hidden_low = low(hidden)
    pre_act = low_back(jnp.einsum('gvd,df->gvf', hidden_low, w_up, precision=HIGHEST)) + up_bias
    act_low = low(jax.nn.gelu(pre_act))
    feed_out = low_back(jnp.einsum('gvf,fd->gvd', act_low, w_down, precision=HIGHEST)) + out_bias[1]
    return norm_rows(hidden + feed_out, norm_gain[1], norm_shift[1]) * live_rows[:, :, None]

def forward(inputs, dataset_bias, w_qkv, qv_bias, w_out, out_bias, w_up, up_bias, w_down, norm_gain, norm_shift, one_hot, live_mask):
    params = (dataset_bias, w_qkv, qv_bias, w_out, out_bias, w_up, up_bias, w_down, norm_gain, norm_shift)
    block_windows = 4
    blocks = WINDOWS // block_windows
    packed = (inputs.reshape(blocks, block_windows, V, D), one_hot.reshape(blocks, block_windows, DATASETS), live_mask.reshape(blocks, block_windows, V))
    results = lax.map(jax.checkpoint(functools.partial(window_block, params)), packed)
    return results.reshape(WINDOWS, V, D)

def reference(inputs, dataset, variate_mask, dataset_bias, w_qkv, qv_bias, w_out, out_bias, w_up, up_bias, w_down, norm_gain, norm_shift, cotangent):
    one_hot = (dataset[:, None] == jnp.arange(DATASETS, dtype=jnp.int32)[None, :]).astype(jnp.float32)
    live_mask = variate_mask.astype(jnp.float32)
    floats = tuple((array_in.astype(jnp.float32) for array_in in (inputs, dataset_bias, w_qkv, qv_bias, w_out, out_bias, w_up, up_bias, w_down, norm_gain, norm_shift)))
    outputs, pullback = jax.vjp(functools.partial(forward, one_hot=one_hot, live_mask=live_mask), *floats)
    gradients = pullback(cotangent.astype(jnp.float32))
    return (outputs.astype(jnp.bfloat16), gradients[0].astype(jnp.bfloat16), gradients[1], gradients[2], gradients[3], gradients[4], gradients[5], gradients[6], gradients[7], gradients[8], gradients[9], gradients[10])
```

```python
import functools
import math

import jax
import jax.numpy as jnp
from jax import lax
from jax.experimental import pallas as pl
from jax.experimental.pallas import tpu as pltpu
from jax.sharding import PartitionSpec as P

HD = 64
EPSILON = 1e-05
NEG_FILL = -1e30
BF = jnp.bfloat16
F32 = jnp.float32
MESH = pl.DeviceIdType.MESH
GELU_C = math.sqrt(2.0 / math.pi)
LANES = 128


def nn(a, b):
    return jnp.dot(a, b, preferred_element_type=F32)


def nt(a, b):
    return lax.dot_general(a, b, (((1,), (1,)), ((), ())), preferred_element_type=F32)


def tn(a, b):
    return lax.dot_general(a, b, (((0,), (0,)), ((), ())), preferred_element_type=F32)


def flip(value, k):
    low = lax.rem(lax.rem(value, 2) + k % 2, 2) if isinstance(k, int) else lax.rem(lax.rem(value, 2) + lax.rem(k, 2), 2)
    high = lax.rem(lax.div(value, 2) + (k // 2 if isinstance(k, int) else lax.div(k, 2)), 2)
    return high * 2 + low


def aligned(index, size):
    return pl.ds(pl.multiple_of(index * size, size), size)


def kernel(
    quad, rest_n,
    x_in, cot_in, dataset, mask, dbias, w_qkv, qvb, w_out, obias, w_up, upb, w_down, gain, shift,
    out_rows, ig_rows, g_qkv, g_out, g_up, g_down, g_dbias, g_gain, g_shift, g_obias, g_upb, g_qvb,
    X, COT, WP, WO, WU, WD, SB, ACT, QA, KA, VA, PR, MIX, LINV, N1, HL, ACT2, GP, ACC, G2L, LIVE,
    G, RC, RX, RQ, RE, SM, SMT, SMQ, SMR,
    s_own, s_x, r_x, s_c, r_c, s_w, r_w, s_b, r_b, s_out, r_out, s_ig, r_ig, s_loc,
    s_rc, r_rc, s_rx, r_rx, s_rq, r_rq, s_re, r_re, s_ag, r_ag, s_sm, r_sm, s_res,
):
    dp = lax.axis_index("dp")
    tp = lax.axis_index("tp")
    q_id = lax.rem(dp, quad)
    r_id = lax.div(dp, quad)
    rows = x_in.shape[1]
    total, width = X.shape
    half = total // 2
    x_id = lax.div(tp, 2)

    def tp_peer(k):
        return (dp, flip(tp, k))

    def quad_at(j):
        return lax.rem(q_id + j + quad, quad)

    def quad_peer(j):
        return (r_id * quad + quad_at(j), tp)

    def rest_peer(j):
        return (lax.rem(r_id + j, rest_n) * quad + q_id, tp)

    def rcopy(src, dst, ss, rs, dev):
        return pltpu.make_async_remote_copy(
            src_ref=src, dst_ref=dst, send_sem=ss, recv_sem=rs, device_id=dev, device_id_type=MESH
        )

    barrier = pltpu.get_barrier_semaphore()
    peers = [tp_peer(k) for k in (1, 2, 3)] + [quad_peer(j) for j in range(1, quad)]
    peers += [rest_peer(j) for j in range(1, rest_n)]
    for peer in peers:
        pl.semaphore_signal(barrier, inc=1, device_id=peer, device_id_type=MESH)

    own = [pltpu.make_async_copy(x_in.at[tp], X.at[aligned(tp, rows), :], s_own.at[0])]
    for i in range(3):
        own.append(pltpu.make_async_copy(w_qkv.at[i], WP.at[tp, :, pl.ds(i * LANES, LANES)], s_own.at[1 + i]))
    own.append(pltpu.make_async_copy(w_out, WO.at[aligned(tp, LANES), :], s_own.at[4]))
    own.append(pltpu.make_async_copy(w_up, WU.at[tp], s_own.at[5]))
    own.append(pltpu.make_async_copy(w_down, WD.at[tp], s_own.at[6]))
    own.append(pltpu.make_async_copy(cot_in.at[tp], COT.at[aligned(tp, rows), :], s_own.at[7]))
    for copy in own:
        copy.start()

    SB[tp, 0:2, :] = qvb[...].astype(F32)
    SB[tp, 2:6, :] = upb[...].astype(F32)
    pl.semaphore_wait(barrier, len(peers))

    def weight_slices(t):
        return [WP.at[t, :, pl.ds(i * LANES, LANES)] for i in range(3)] + [
            WO.at[aligned(t, LANES), :], WU.at[t], WD.at[t]
        ]

    w_src = [w_qkv.at[0], w_qkv.at[1], w_qkv.at[2], w_out, w_up, w_down]
    w_dst = weight_slices(tp)

    def w_send(i, k):
        return rcopy(w_src[i], w_dst[i], s_w.at[i, k], r_w.at[i, k], tp_peer(k))

    def w_wait(i, k):
        dst = weight_slices(flip(tp, k))[i]
        rcopy(dst, dst, s_w.at[i, k], r_w.at[i, k], tp_peer(k)).wait_recv()

    def w_forward(i):
        dst = weight_slices(flip(tp, 2))[i]
        return rcopy(dst, dst, s_w.at[i, 3], r_w.at[i, 3], tp_peer(1))

    def rows_copy(src, dst, ss, rs, k):
        return rcopy(src.at[flip(tp, k)], dst.at[aligned(tp, rows), :], ss.at[k], rs.at[k], tp_peer(k))

    def rows_wait(dst, ss, rs, k):
        there = dst.at[aligned(flip(tp, k), rows), :]
        rcopy(there, there, ss.at[k], rs.at[k], tp_peer(k)).wait_recv()

    def sb_copy(k):
        return rcopy(SB.at[tp], SB.at[tp], s_b.at[k], r_b.at[k], tp_peer(k))

    sends = []
    for k in (1, 2, 3):
        sends.append(sb_copy(k))
    for i in range(3):
        sends.append(w_send(i, 2))
        sends.append(w_send(i, 1))
    for k in (2, 3, 1):
        sends.append(rows_copy(x_in, X, s_x, r_x, k))
    for i in (3, 4, 5):
        sends.append(w_send(i, 2))
        sends.append(w_send(i, 1))
    for k in (2, 3, 1):
        sends.append(rows_copy(cot_in, COT, s_c, r_c, k))
    for copy in sends:
        copy.start()

    live_row = mask[pl.ds(tp, 1), :].astype(F32)
    LIVE[:, 0:8] = jnp.transpose(jnp.broadcast_to(live_row, (8, total)))
    ds_here = dataset[tp]
    off = jnp.zeros((1, X.shape[1]), F32)
    for c in range(dbias.shape[0]):
        off = off + jnp.where(ds_here == c, 1.0, 0.0) * dbias[c : c + 1, :].astype(F32)

    for copy in own:
        copy.wait()
    for k in (1, 2, 3):
        there = SB.at[flip(tp, k)]
        rcopy(there, there, s_b.at[k], r_b.at[k], tp_peer(k)).wait_recv()

    lane = lax.broadcasted_iota(jnp.int32, (half, LANES), 1)
    upper = lane >= HD
    one = jnp.ones((), BF)
    zero = jnp.zeros((), BF)

    def project(hh, first):
        rr = aligned(hh, half)
        ACT[rr, :] = (X[rr, :].astype(F32) + off).astype(BF)
        fill = jnp.where(LIVE[rr, 0:1] > 0.5, 0.0, NEG_FILL).astype(BF)
        fill = jnp.broadcast_to(fill, (half, LANES))

        def shard(k, carry):
            t = flip(tp, k)
            if first:
                @pl.when(k == 1)
                def _():
                    for i in range(3):
                        w_wait(i, 1)

                @pl.when(k == 2)
                def _():
                    for i in range(3):
                        w_wait(i, 2)
                        w_forward(i).start()

                @pl.when(k == 3)
                def _():
                    for i in range(3):
                        w_wait(i, 3)

            qkv = nn(ACT[rr, :], WP[t])
            query = (qkv[:, :LANES] + SB[t, 0:1, :]).astype(BF) * BF(0.125)
            keys = qkv[:, LANES : 2 * LANES].astype(BF)
            vals = (qkv[:, 2 * LANES :] + SB[t, 1:2, :]).astype(BF)
            QA[2 * t, rr, :] = jnp.where(upper, jnp.where(lane == HD, one, zero), query)
            QA[2 * t + 1, rr, :] = jnp.where(upper, query, jnp.where(lane == 0, one, zero))
            KA[2 * t, rr, :] = jnp.where(upper, jnp.where(lane == HD, fill, zero), keys)
            KA[2 * t + 1, rr, :] = jnp.where(upper, keys, jnp.where(lane == 0, fill, zero))
            VA[2 * t, rr, :] = jnp.where(upper, -one, vals)
            VA[2 * t + 1, rr, :] = jnp.where(upper, vals, -one)
            return carry

        lax.fori_loop(0, 4, shard, 0)

    rows_wait(X, s_x, r_x, 1)
    project(x_id, True)
    rows_wait(X, s_x, r_x, 2)
    rows_wait(X, s_x, r_x, 3)
    project(1 - x_id, False)

    def attend(p, carry):
        for c in range(2):
            rr = pl.ds(c * half, half)
            outs = []
            for e in range(2):
                h = 2 * p + e
                scores = nt(QA[h, rr, :], KA[h])
                top = jnp.max(scores, axis=1, keepdims=True)
                weight = jnp.exp(scores - top).astype(BF)
                PR[h, rr, :] = weight
                outs.append(nn(weight, VA[h]))
            inv = -1.0 / jnp.where(upper, pltpu.roll(outs[1], HD, 1), pltpu.roll(outs[0], HD, 1))
            LINV[p, rr, :] = inv
            MIX[p, rr, :] = (jnp.where(upper, outs[1], outs[0]) * inv).astype(BF)
        return carry

    lax.fori_loop(0, 4, attend, 0)

    for i in (3, 4, 5):
        w_wait(i, 2)
        w_forward(i).start()
    w_wait(3, 1)
    w_wait(3, 3)

    acc = nn(MIX[0], WO[0:LANES, :])
    for p in range(1, 4):
        acc = acc + nn(MIX[p], WO[p * LANES : (p + 1) * LANES, :])
    ACC[...] = acc

    step = total // 8
    gain0, gain1 = gain[0:1, :].astype(F32), gain[1:2, :].astype(F32)
    shift0, shift1 = shift[0:1, :].astype(F32), shift[1:2, :].astype(F32)
    ob0, ob1 = obias[0:1, :].astype(F32), obias[1:2, :].astype(F32)

    def norm_one(i, carry):
        rr = aligned(i, step)
        res = X[rr, :].astype(F32) + off + (ACC[rr, :] + ob0)
        cen = res - jnp.mean(res, axis=-1, keepdims=True)
        fac = lax.rsqrt(jnp.mean(cen * cen, axis=-1, keepdims=True) + EPSILON)
        nrm = cen * fac
        N1[rr, :] = nrm
        LIVE[rr, 1:2] = fac
        HL[rr, :] = (nrm * gain0 + shift0).astype(BF)
        return carry

    lax.fori_loop(0, 8, norm_one, 0)

    ACC[...] = jnp.zeros_like(ACC)

    def ffn(k, carry):
        t = flip(tp, k)

        @pl.when(k == 1)
        def _():
            w_wait(4, 1)
            w_wait(5, 1)

        @pl.when(k == 3)
        def _():
            w_wait(4, 3)
            w_wait(5, 3)

        for c in range(2):
            rr = pl.ds(c * half, half)
            upper_bias = jnp.concatenate([SB[t, 2 + i : 3 + i, :] for i in range(4)], axis=1)
            u = nn(HL[rr, :], WU[t]) + upper_bias
            sq = u * u
            th = jnp.tanh(u * (GELU_C + (GELU_C * 0.044715) * sq))
            hp = 0.5 + 0.5 * th
            act = (u * hp).astype(BF)
            ACT2[t, rr, :] = act
            GP[t, rr, :] = (
                hp + (0.5 * u) * (1.0 - th * th) * (GELU_C + (3.0 * GELU_C * 0.044715) * sq)
            ).astype(BF)
            ACC[rr, :] += nn(act, WD[t])
        return carry

    lax.fori_loop(0, 4, ffn, 0)

    for k in (1, 2, 3):
        rows_wait(COT, s_c, r_c, k)

    SM[...] = jnp.zeros_like(SM)

    def norm_two(i, carry):
        rr = aligned(i, step)
        hid = N1[rr, :] * gain0 + shift0
        res = hid + (ACC[rr, :] + ob1)
        cen = res - jnp.mean(res, axis=-1, keepdims=True)
        fac = lax.rsqrt(jnp.mean(cen * cen, axis=-1, keepdims=True) + EPSILON)
        nrm = cen * fac
        live = LIVE[rr, 0:1]
        gf = COT[rr, :].astype(F32) * live
        COT[rr, :] = ((nrm * gain1 + shift1) * live).astype(BF)
        gn = gf * gain1
        g2 = fac * (
            gn - jnp.mean(gn, axis=-1, keepdims=True) - nrm * jnp.mean(gn * nrm, axis=-1, keepdims=True)
        )
        ACC[rr, :] = g2
        G2L[rr, :] = g2.astype(BF)
        SM[5:6, :] += jnp.sum(gf * nrm, axis=0, keepdims=True)
        SM[7:8, :] += jnp.sum(gf, axis=0, keepdims=True)
        SM[9:10, :] += jnp.sum(g2, axis=0, keepdims=True)
        return carry

    lax.fori_loop(0, 8, norm_two, 0)

    def back_copy(buf, dst, ss, rs, k):
        return rcopy(buf.at[aligned(flip(tp, k), rows), :], dst.at[tp], ss.at[k], rs.at[k], tp_peer(k))

    def back_wait(buf, dst, ss, rs, k):
        there = dst.at[flip(tp, k)]
        rcopy(buf.at[aligned(tp, rows), :], there, ss.at[k], rs.at[k], tp_peer(k)).wait_recv()

    outs_sent = [back_copy(COT, out_rows, s_out, r_out, k) for k in (2, 3, 1)]
    for copy in outs_sent:
        copy.start()
    out_local = pltpu.make_async_copy(COT.at[aligned(tp, rows), :], out_rows.at[tp], s_loc.at[0])
    out_local.start()

    def gref(m, t):
        return WU.at[t] if m == 2 else G.at[m, t]

    def core_send(m, j):
        k = 1 if j == 0 else 3
        return rcopy(gref(m, flip(tp, k)), RC.at[m, j], s_rc.at[m, j], r_rc.at[m, j], tp_peer(1))

    def core_wait(m, j):
        rcopy(RC.at[m, j], RC.at[m, j], s_rc.at[m, j], r_rc.at[m, j], tp_peer(1)).wait_recv()

    def x_send(m):
        return rcopy(gref(m, flip(tp, 2)), RX.at[m], s_rx.at[m], r_rx.at[m], tp_peer(2))

    def reduce_early(m, k):
        @pl.when(k == 0)
        def _():
            core_send(m, 1).start()

        @pl.when(k == 1)
        def _():
            core_wait(m, 1)
            t = flip(tp, 2)
            ref = gref(m, t)
            ref[...] = (ref[...].astype(F32) + RC[m, 1].astype(F32)).astype(BF)
            x_send(m).start()

        @pl.when(k == 2)
        def _():
            core_send(m, 0).start()

    qrows = 512 // quad

    def quad_send(m, j):
        return rcopy(
            gref(m, tp).at[aligned(quad_at(j), qrows), :], RQ.at[m, j - 1], s_rq.at[m, j - 1], r_rq.at[m, j - 1],
            quad_peer(j),
        )

    def rest_send(m, j):
        return rcopy(RE.at[m, r_id], RE.at[m, r_id], s_re.at[m, j - 1], r_re.at[m, j - 1], rest_peer(j))

    def rest_wait(m, j):
        there = RE.at[m, lax.rem(r_id + rest_n - j, rest_n)]
        rcopy(there, there, s_re.at[m, j - 1], r_re.at[m, j - 1], rest_peer(j)).wait_recv()

    def ag_send(m, j):
        here = RX.at[m, aligned(q_id, qrows), :]
        return rcopy(here, here, s_ag.at[m, j - 1], r_ag.at[m, j - 1], quad_peer(j))

    def ag_wait(m, j):
        there = RX.at[m, aligned(quad_at(-j), qrows), :]
        rcopy(there, there, s_ag.at[m, j - 1], r_ag.at[m, j - 1], quad_peer(j)).wait_recv()

    def reduce_quad(m):
        core_wait(m, 0)
        rcopy(RX.at[m], RX.at[m], s_rx.at[m], r_rx.at[m], tp_peer(2)).wait_recv()
        ref = gref(m, tp)
        ref[...] = (ref[...].astype(F32) + RC[m, 0].astype(F32) + RX[m].astype(F32)).astype(BF)
        for j in range(1, quad):
            quad_send(m, j).start()

    def reduce_rest(m):
        for j in range(1, quad):
            quad_send(m, j).wait_recv()
        acc_q = gref(m, tp)[aligned(q_id, qrows), :].astype(F32)
        for j in range(quad - 1):
            acc_q = acc_q + RQ[m, j].astype(F32)
        RE[m, r_id] = acc_q.astype(BF)
        for j in range(1, rest_n):
            rest_send(m, j).start()

    def reduce_gather(m):
        for j in range(1, rest_n):
            rest_wait(m, j)
        acc_r = RE[m, 0].astype(F32)
        for j in range(1, rest_n):
            acc_r = acc_r + RE[m, j].astype(F32)
        RX[m, aligned(q_id, qrows), :] = acc_r.astype(BF)
        for j in range(1, quad):
            ag_send(m, j).start()

    def reduce_done(m):
        for j in range(1, quad):
            ag_wait(m, j)


    def ffn_back(k, carry):
        t = flip(tp, 3 - k)
        d_act = nt(G2L[...], WD[t])
        g_pre = d_act * GP[t].astype(F32)
        SM[pl.ds(10 + t, 1), :] = jnp.sum(g_pre, axis=0, keepdims=True)
        low = g_pre.astype(BF)
        GP[t] = low
        G[0, t] = tn(ACT2[t], G2L[...]).astype(BF)
        G[1, t] = tn(HL[...], low).astype(BF)
        ACC[...] += nt(low, WU[t])
        reduce_early(0, k)
        reduce_early(1, k)
        return carry

    lax.fori_loop(0, 4, ffn_back, 0)

    def norm_one_back(i, carry):
        rr = aligned(i, step)
        gh = ACC[rr, :]
        nrm = N1[rr, :]
        gn = gh * gain0
        g1 = LIVE[rr, 1:2] * (
            gn - jnp.mean(gn, axis=-1, keepdims=True) - nrm * jnp.mean(gn * nrm, axis=-1, keepdims=True)
        )
        ACC[rr, :] = g1
        G2L[rr, :] = g1.astype(BF)
        SM[4:5, :] += jnp.sum(gh * nrm, axis=0, keepdims=True)
        SM[6:7, :] += jnp.sum(gh, axis=0, keepdims=True)
        SM[8:9, :] += jnp.sum(g1, axis=0, keepdims=True)
        return carry

    lax.fori_loop(0, 8, norm_one_back, 0)

    def back_prep(p, carry):
        gm = nt(G2L[...], WO[aligned(p, LANES), :])
        WU[p, pl.ds(3 * LANES, LANES), :] = tn(MIX[p], G2L[...]).astype(BF)
        lane_f = lax.broadcasted_iota(jnp.int32, (total, LANES), 1)
        up_f = lane_f >= HD
        gs = gm * LINV[p]
        prod = gs * MIX[p].astype(F32)
        low = gs.astype(BF)
        for e in range(2):
            mine = up_f if e == 1 else jnp.logical_not(up_f)
            delta = jnp.sum(jnp.where(mine, prod, 0.0), axis=-1, keepdims=True)
            hi = delta.astype(BF)
            lo = (delta - hi.astype(F32)).astype(BF)
            base = HD * (1 - e)
            side = jnp.where(lane_f == base, hi, jnp.where(lane_f == base + 1, lo, zero))
            GP[p, :, pl.ds(e * LANES, LANES)] = jnp.where(mine, low, side)
        return carry

    w_forward(4).wait_send()
    lax.fori_loop(0, 4, back_prep, 0)

    ones = jnp.ones((8, total), BF)
    lane_f = lax.broadcasted_iota(jnp.int32, (total, LANES), 1)
    up_f = lane_f >= HD

    def attend_back(k, carry):
        p = flip(tp, 3 - k)
        d_k, d_v = [], []
        for c in range(2):
            rr = pl.ds(c * half, half)
            part = []
            for e in range(2):
                h = 2 * p + e
                go = GP[p, rr, pl.ds(e * LANES, LANES)]
                prob = PR[h, rr, :]
                d_s = (prob.astype(F32) * nt(go, VA[h])).astype(BF)
                part.append(nn(d_s, KA[h]))
                more = (tn(prob, go), tn(d_s, QA[h, rr, :]))
                if c == 0:
                    d_v.append(more[0])
                    d_k.append(more[1])
                else:
                    d_v[e] = d_v[e] + more[0]
                    d_k[e] = d_k[e] + more[1]
            ACT2[p, rr, 0:LANES] = (jnp.where(upper, part[1], part[0]) * 0.125).astype(BF)
        ACT2[p, :, LANES : 2 * LANES] = jnp.where(up_f, d_k[1], d_k[0]).astype(BF)
        ACT2[p, :, 2 * LANES : 3 * LANES] = jnp.where(up_f, d_v[1], d_v[0]).astype(BF)
        d_all = ACT2[p, :, 0 : 3 * LANES]
        WU[p, 0 : 3 * LANES, :] = tn(d_all, ACT[...]).astype(BF)
        sums = nn(ones, d_all)
        SM[14:15, aligned(p, LANES)] = sums[0:1, 0:LANES]
        SM[15:16, aligned(p, LANES)] = sums[0:1, 2 * LANES : 3 * LANES]
        reduce_early(2, k)

        @pl.when(k == 1)
        def _():
            reduce_quad(0)

        @pl.when(k == 2)
        def _():
            reduce_quad(1)

        @pl.when(k == 3)
        def _():
            reduce_rest(0)

        return carry

    lax.fori_loop(0, 4, attend_back, 0)

    reduce_quad(2)
    reduce_rest(1)
    reduce_gather(0)

    def input_grad(k, carry):
        b = flip(tp, 3 - k)
        rr = aligned(b, rows)
        grad = ACC[rr, :]
        for p in range(4):
            grad = grad + nt(ACT2[p, rr, 0 : 3 * LANES], WP[p])
        X[rr, :] = grad.astype(BF)
        SM[0:1, :] += jnp.sum(grad, axis=0, keepdims=True)

        @pl.when(k < 3)
        def _():
            kk = 3 - k
            rcopy(X.at[rr, :], ig_rows.at[tp], s_ig.at[kk], r_ig.at[kk], (dp, b)).start()

        return carry

    lax.fori_loop(0, 4, input_grad, 0)
    ig_local = pltpu.make_async_copy(X.at[aligned(tp, rows), :], ig_rows.at[tp], s_loc.at[1])
    ig_local.start()

    base_sum = SM[0:1, :]
    for c in range(dbias.shape[0]):
        SM[c : c + 1, :] = jnp.where(ds_here == c, 1.0, 0.0) * base_sum

    def sm_all(src, slots, me, count, sem0, peer_of, from_of):
        slots[me] = src
        copies = []
        for j in range(1, count):
            copies.append(rcopy(slots.at[me], slots.at[me], s_sm.at[sem0 + j], r_sm.at[sem0 + j], peer_of(j)))
        for copy in copies:
            copy.start()
        for j in range(1, count):
            there = slots.at[from_of(j)]
            rcopy(there, there, s_sm.at[sem0 + j], r_sm.at[sem0 + j], peer_of(j)).wait_recv()
        out = slots[0]
        for j in range(1, count):
            out = out + slots[j]
        return out, copies

    reduce_rest(2)
    reduce_gather(1)
    val, c1 = sm_all(SM[...], SMT, tp, 4, 0, tp_peer, lambda j: flip(tp, j))
    val, c2 = sm_all(val, SMQ, q_id, quad, 4, quad_peer, lambda j: quad_at(-j))
    reduce_gather(2)
    val, c3 = sm_all(val, SMR, r_id, rest_n, 4 + quad, rest_peer, lambda j: lax.rem(r_id + rest_n - j, rest_n))
    SM[...] = val
    g_dbias[...] = val[0:4, :]
    g_gain[...] = val[4:6, :]
    g_shift[...] = val[6:8, :]
    g_obias[...] = val[8:10, :]
    g_upb[...] = SM[pl.ds(10 + tp, 1), :]
    g_qvb[...] = SM[14:16, aligned(tp, LANES)]

    results = []

    def result(src, dst, i):
        results.append(pltpu.make_async_copy(src, dst, s_res.at[i]))
        results[-1].start()

    reduce_done(0)
    N1[0:width, :] = RX[0].astype(F32)
    result(N1.at[0:width, :], g_down, 0)
    reduce_done(1)
    ACC[0:width, :] = RX[1].astype(F32)
    result(ACC.at[0:width, :], g_up, 1)
    reduce_done(2)
    for i in range(3):
        LINV[i, 0:width, :] = jnp.transpose(RX[2, i * LANES : (i + 1) * LANES, :].astype(F32))
        result(LINV.at[i, 0:width, :], g_qkv.at[i], 2 + i)
    N1[width : width + LANES, :] = RX[2, 3 * LANES : 4 * LANES, :].astype(F32)
    result(N1.at[width : width + LANES, :], g_out, 5)
    for copy in results:
        copy.wait()

    for k in (1, 2, 3):
        back_wait(COT, out_rows, s_out, r_out, k)
        back_wait(X, ig_rows, s_ig, r_ig, k)
        back_copy(X, ig_rows, s_ig, r_ig, k).wait_send()
    ig_local.wait()
    out_local.wait()
    for copy in sends + outs_sent + c1 + c2 + c3:
        copy.wait_send()
    for i in (0, 1, 2, 3, 5):
        w_forward(i).wait_send()
    for m in range(3):
        core_send(m, 0).wait_send()
        core_send(m, 1).wait_send()
        x_send(m).wait_send()
        for j in range(1, quad):
            quad_send(m, j).wait_send()
            ag_send(m, j).wait_send()
        for j in range(1, rest_n):
            rest_send(m, j).wait_send()


def shards(dp_n, *args):
    (inputs, dataset, variate_mask, dataset_bias, w_qkv, qv_bias, w_out, out_bias, w_up, up_bias, w_down,
     norm_gain, norm_shift, cotangent) = args
    win, rows, width = inputs.shape
    total = variate_mask.shape[1]
    quad = 4 if dp_n <= 16 else 8
    rest_n = dp_n // quad
    ffs = w_up.shape[1]
    assert win == 4 and total == 4 * rows and width == 512 and ffs == 512 and w_out.shape[0] == LANES
    any_spec = pl.BlockSpec(memory_space=pl.ANY)
    vmem = pl.BlockSpec(memory_space=pltpu.VMEM)
    smem = pl.BlockSpec(memory_space=pltpu.SMEM)
    dma = pltpu.SemaphoreType.DMA
    V = pltpu.VMEM
    scratch = [
        V((total, width), BF),
        V((total, width), BF),
        V((4, width, 3 * LANES), BF),
        V((width, width), BF),
        V((4, width, ffs), BF),
        V((4, ffs, width), BF),
        V((4, 8, LANES), F32),
        V((total, width), BF),
        V((8, total, LANES), BF),
        V((8, total, LANES), BF),
        V((8, total, LANES), BF),
        V((8, total, total), BF),
        V((4, total, LANES), BF),
        V((4, total, LANES), F32),
        V((total, width), F32),
        V((total, width), BF),
        V((4, total, ffs), BF),
        V((4, total, ffs), BF),
        V((total, width), F32),
        V((total, width), BF),
        V((total, LANES), F32),
        V((2, 4, width, ffs), BF),
        V((3, 2, width, ffs), BF),
        V((3, width, ffs), BF),
        V((3, quad - 1, width // quad, ffs), BF),
        V((3, rest_n, width // quad, ffs), BF),
        V((16, width), F32),
        V((4, 16, width), F32),
        V((quad, 16, width), F32),
        V((rest_n, 16, width), F32),
        dma((8,)),
        dma((4,)), dma((4,)),
        dma((4,)), dma((4,)),
        dma((6, 4)), dma((6, 4)),
        dma((4,)), dma((4,)),
        dma((4,)), dma((4,)),
        dma((4,)), dma((4,)),
        dma((2,)),
        dma((3, 2)), dma((3, 2)),
        dma((3,)), dma((3,)),
        dma((3, quad - 1)), dma((3, quad - 1)),
        dma((3, max(rest_n - 1, 1))), dma((3, max(rest_n - 1, 1))),
        dma((3, quad - 1)), dma((3, quad - 1)),
        dma((4 + quad + rest_n,)), dma((4 + quad + rest_n,)),
        dma((6,)),
    ]
    sds = jax.ShapeDtypeStruct
    outs = pl.pallas_call(
        functools.partial(kernel, quad, rest_n),
        out_shape=(
            sds((win, rows, width), BF),
            sds((win, rows, width), BF),
            sds((3, width, LANES), F32),
            sds((LANES, width), F32),
            sds((width, ffs), F32),
            sds((ffs, width), F32),
            sds((4, width), F32),
            sds((2, width), F32),
            sds((2, width), F32),
            sds((2, width), F32),
            sds((1, width), F32),
            sds((2, LANES), F32),
        ),
        in_specs=[any_spec, any_spec, smem, vmem, vmem, any_spec, vmem, any_spec, vmem, any_spec, vmem, any_spec, vmem, vmem],
        out_specs=(any_spec,) * 6 + (vmem,) * 6,
        scratch_shapes=scratch,
        compiler_params=pltpu.CompilerParams(
            collective_id=0, has_side_effects=True, vmem_limit_bytes=65000000
        ),
        cost_estimate=pl.CostEstimate(flops=30 * 10**9, bytes_accessed=20 * 10**6, transcendentals=10**7),
        name="encoder_layer",
    )(inputs, cotangent, dataset, variate_mask, dataset_bias, w_qkv, qv_bias, w_out, out_bias, w_up,
      up_bias.reshape(4, LANES), w_down, norm_gain, norm_shift)
    (rows_out, rows_ig, g_qkv, g_out, g_up, g_down, g_dbias, g_gain, g_shift, g_obias, g_upb, g_qvb) = outs
    return (
        rows_out, rows_ig, g_dbias, g_qkv, g_qvb, g_out, g_obias, g_up, g_upb.reshape(-1), g_down, g_gain, g_shift,
    )


def solution(mesh):
    in_specs = (
        P("dp", "tp", None), P("dp"), P("dp", None), P(), P(None, None, "tp"), P(None, "tp"), P("tp", None), P(),
        P(None, "tp"), P("tp"), P("tp", None), P(), P(), P("dp", "tp", None),
    )
    out_specs = (
        P("dp", "tp", None), P("dp", "tp", None), P(), P(None, None, "tp"), P(None, "tp"), P("tp", None), P(),
        P(None, "tp"), P("tp"), P("tp", None), P(), P(),
    )
    body = functools.partial(shards, mesh.shape["dp"])
    return jax.shard_map(body, mesh=mesh, in_specs=in_specs, out_specs=out_specs, check_vma=False)
```

```python
import functools
import math

import jax
import jax.numpy as jnp
from jax import lax
from jax.experimental import pallas as pl
from jax.experimental.pallas import tpu as pltpu
from jax.sharding import PartitionSpec as P

HD = 64
EPSILON = 1e-05
NEG_FILL = -1e30
BF = jnp.bfloat16
F32 = jnp.float32
MESH = pl.DeviceIdType.MESH
GELU_C = math.sqrt(2.0 / math.pi)
LANES = 128


def nn(a, b):
    return jnp.dot(a, b, preferred_element_type=F32)


def nt(a, b):
    return lax.dot_general(a, b, (((1,), (1,)), ((), ())), preferred_element_type=F32)


def tn(a, b):
    return lax.dot_general(a, b, (((0,), (0,)), ((), ())), preferred_element_type=F32)


def flip(value, k):
    low = lax.rem(lax.rem(value, 2) + k % 2, 2) if isinstance(k, int) else lax.rem(lax.rem(value, 2) + lax.rem(k, 2), 2)
    high = lax.rem(lax.div(value, 2) + (k // 2 if isinstance(k, int) else lax.div(k, 2)), 2)
    return high * 2 + low


def aligned(index, size):
    return pl.ds(pl.multiple_of(index * size, size), size)


def kernel(
    quad, rest_n,
    x_in, cot_in, dataset, mask, dbias, w_qkv, qvb, w_out, obias, w_up, upb, w_down, gain, shift,
    out_rows, ig_rows, g_sum, g_small,
    X, COT, WP, WO, WU, WD, SB, ACT, QA, KA, VA, PR, MIX, LINV, N1, HL, ACT2, GP, ACC, G2L, LIVE,
    G, RC, RX, RQ, RE, SM, SMT, SMQ, SMR,
    s_own, s_x, r_x, s_c, r_c, s_wx, r_wx, s_wq, r_wq, s_wf, r_wf, s_wc, r_wc, s_b, r_b, s_out, r_out, s_ig, r_ig, s_loc,
    s_rc, r_rc, s_rx, r_rx, s_rq, r_rq, s_re, r_re, s_ag, r_ag, s_sm, r_sm, s_res,
):
    dp = lax.axis_index("dp")
    tp = lax.axis_index("tp")
    q_id = lax.rem(dp, quad)
    r_id = lax.div(dp, quad)
    rows = x_in.shape[1]
    total, width = X.shape
    half = total // 2
    x_id = lax.div(tp, 2)

    def tp_peer(k):
        return (dp, flip(tp, k))

    def quad_at(j):
        return lax.rem(q_id + j + quad, quad)

    def quad_peer(j):
        return (r_id * quad + quad_at(j), tp)

    def rest_peer(j):
        return (lax.rem(r_id + j, rest_n) * quad + q_id, tp)

    def rcopy(src, dst, ss, rs, dev):
        return pltpu.make_async_remote_copy(
            src_ref=src, dst_ref=dst, send_sem=ss, recv_sem=rs, device_id=dev, device_id_type=MESH
        )

    barrier = pltpu.get_barrier_semaphore()
    peers = [tp_peer(k) for k in (1, 2, 3)] + [quad_peer(j) for j in range(1, quad)]
    peers += [rest_peer(j) for j in range(1, rest_n)]
    for peer in peers:
        pl.semaphore_signal(barrier, inc=1, device_id=peer, device_id_type=MESH)

    own = [pltpu.make_async_copy(x_in.at[tp], X.at[aligned(tp, rows), :], s_own.at[0])]
    for i in range(3):
        own.append(pltpu.make_async_copy(w_qkv.at[i], WP.at[tp, :, pl.ds(i * LANES, LANES)], s_own.at[1 + i]))
    own.append(pltpu.make_async_copy(w_out, WO.at[aligned(tp, LANES), :], s_own.at[4]))
    own.append(pltpu.make_async_copy(w_up, WU.at[tp], s_own.at[5]))
    own.append(pltpu.make_async_copy(w_down, WD.at[tp], s_own.at[6]))
    own.append(pltpu.make_async_copy(cot_in.at[tp], COT.at[aligned(tp, rows), :], s_own.at[7]))
    for copy in own:
        copy.start()

    SB[tp, 0:2, :] = qvb[...].astype(F32)
    SB[tp, 2:6, :] = upb[...].astype(F32)
    pl.semaphore_wait(barrier, len(peers))

    wq = width // quad
    oq = LANES // quad

    def w_whole(g, t):
        return (WP.at[t], WO.at[aligned(t, LANES), :], WU.at[t], WD.at[t])[g]

    def w_part(g, t, q):
        if g == 1:
            return WO.at[pl.ds(pl.multiple_of(t * LANES + q * oq, oq), oq), :]
        return (WP, WO, WU, WD)[g].at[t, aligned(q, wq), :]

    def wx_dst(i, t):
        if i < 3:
            return WP.at[t, aligned(q_id, wq), pl.ds(i * LANES, LANES)]
        return w_part(i - 2, t, q_id)

    wx_src = [w_qkv.at[i, aligned(q_id, wq), :] for i in range(3)]
    wx_src += [w_out.at[aligned(q_id, oq), :], w_up.at[aligned(q_id, wq), :], w_down.at[aligned(q_id, wq), :]]
    members = {0: (0, 1, 2), 1: (3,), 2: (4,), 3: (5,)}

    def wx_send(i):
        return rcopy(wx_src[i], wx_dst(i, tp), s_wx.at[i], r_wx.at[i], tp_peer(2))

    def wx_wait(g):
        for i in members[g]:
            there = wx_dst(i, flip(tp, 2))
            rcopy(there, there, s_wx.at[i], r_wx.at[i], tp_peer(2)).wait_recv()

    def wq_send(g, j):
        here = w_part(g, flip(tp, 2), q_id)
        return rcopy(here, here, s_wq.at[g, j - 1], r_wq.at[g, j - 1], quad_peer(j))

    def wq_start(g):
        wx_wait(g)
        for j in range(1, quad):
            wq_send(g, j).start()

    def wf_send(g):
        here = w_whole(g, flip(tp, 2))
        return rcopy(here, here, s_wf.at[g], r_wf.at[g], tp_peer(1))

    def wf_start(g):
        for j in range(1, quad):
            there = w_part(g, flip(tp, 2), quad_at(-j))
            rcopy(there, there, s_wq.at[g, j - 1], r_wq.at[g, j - 1], quad_peer(j)).wait_recv()
        wf_send(g).start()

    def wf_wait(g):
        there = w_whole(g, flip(tp, 3))
        rcopy(there, there, s_wf.at[g], r_wf.at[g], tp_peer(1)).wait_recv()

    def wc_dst(i, t):
        return WP.at[t, :, pl.ds(i * LANES, LANES)] if i < 3 else w_whole(i - 2, t)

    wc_src = [w_qkv.at[0], w_qkv.at[1], w_qkv.at[2], w_out, w_up, w_down]

    def wc_send(i):
        return rcopy(wc_src[i], wc_dst(i, tp), s_wc.at[i], r_wc.at[i], tp_peer(1))

    def wc_wait(g):
        for i in members[g]:
            there = wc_dst(i, flip(tp, 1))
            rcopy(there, there, s_wc.at[i], r_wc.at[i], tp_peer(1)).wait_recv()

    def rows_copy(src, dst, ss, rs, k):
        return rcopy(src.at[flip(tp, k)], dst.at[aligned(tp, rows), :], ss.at[k], rs.at[k], tp_peer(k))

    def rows_wait(dst, ss, rs, k):
        there = dst.at[aligned(flip(tp, k), rows), :]
        rcopy(there, there, ss.at[k], rs.at[k], tp_peer(k)).wait_recv()

    def sb_copy(k):
        return rcopy(SB.at[tp], SB.at[tp], s_b.at[k], r_b.at[k], tp_peer(k))

    sends = []
    for k in (1, 2, 3):
        sends.append(sb_copy(k))
    for i in range(4):
        sends.append(wx_send(i))
    for i in range(4):
        sends.append(wc_send(i))
    for k in (2, 3, 1):
        sends.append(rows_copy(x_in, X, s_x, r_x, k))
    for i in (4, 5):
        sends.append(wx_send(i))
        sends.append(wc_send(i))
    for k in (2, 3, 1):
        sends.append(rows_copy(cot_in, COT, s_c, r_c, k))
    for copy in sends:
        copy.start()

    live_row = mask[pl.ds(tp, 1), :].astype(F32)
    LIVE[:, 0:8] = jnp.transpose(jnp.broadcast_to(live_row, (8, total)))
    ds_here = dataset[tp]
    off = jnp.zeros((1, X.shape[1]), F32)
    for c in range(dbias.shape[0]):
        off = off + jnp.where(ds_here == c, 1.0, 0.0) * dbias[c : c + 1, :].astype(F32)

    for copy in own:
        copy.wait()
    for k in (1, 2, 3):
        there = SB.at[flip(tp, k)]
        rcopy(there, there, s_b.at[k], r_b.at[k], tp_peer(k)).wait_recv()

    lane = lax.broadcasted_iota(jnp.int32, (half, LANES), 1)
    upper = lane >= HD
    one = jnp.ones((), BF)
    zero = jnp.zeros((), BF)

    def project(hh, first):
        rr = aligned(hh, half)
        ACT[rr, :] = (X[rr, :].astype(F32) + off).astype(BF)
        fill = jnp.where(LIVE[rr, 0:1] > 0.5, 0.0, NEG_FILL).astype(BF)
        fill = jnp.broadcast_to(fill, (half, LANES))

        def shard(k, carry):
            t = flip(tp, k)
            if first:
                @pl.when(k == 1)
                def _():
                    wc_wait(0)

                @pl.when(k == 2)
                def _():
                    wf_start(0)
                    wf_start(1)

                @pl.when(k == 3)
                def _():
                    wf_wait(0)

            qkv = nn(ACT[rr, :], WP[t])
            query = (qkv[:, :LANES] + SB[t, 0:1, :]).astype(BF) * BF(0.125)
            keys = qkv[:, LANES : 2 * LANES].astype(BF)
            vals = (qkv[:, 2 * LANES :] + SB[t, 1:2, :]).astype(BF)
            QA[2 * t, rr, :] = jnp.where(upper, jnp.where(lane == HD, one, zero), query)
            QA[2 * t + 1, rr, :] = jnp.where(upper, query, jnp.where(lane == 0, one, zero))
            KA[2 * t, rr, :] = jnp.where(upper, jnp.where(lane == HD, fill, zero), keys)
            KA[2 * t + 1, rr, :] = jnp.where(upper, keys, jnp.where(lane == 0, fill, zero))
            VA[2 * t, rr, :] = jnp.where(upper, -one, vals)
            VA[2 * t + 1, rr, :] = jnp.where(upper, vals, -one)
            return carry

        lax.fori_loop(0, 4, shard, 0)

    wq_start(0)
    wq_start(1)
    rows_wait(X, s_x, r_x, 1)
    project(x_id, True)
    rows_wait(X, s_x, r_x, 2)
    rows_wait(X, s_x, r_x, 3)
    project(1 - x_id, False)

    def attend(p, carry):
        @pl.when(p == 2)
        def _():
            wq_start(2)
            wq_start(3)

        for c in range(2):
            rr = pl.ds(c * half, half)
            outs = []
            for e in range(2):
                h = 2 * p + e
                scores = nt(QA[h, rr, :], KA[h])
                top = jnp.max(scores, axis=1, keepdims=True)
                weight = jnp.exp(scores - top).astype(BF)
                PR[h, rr, :] = weight
                outs.append(nn(weight, VA[h]))
            inv = -1.0 / jnp.where(upper, pltpu.roll(outs[1], HD, 1), pltpu.roll(outs[0], HD, 1))
            LINV[p, rr, :] = inv
            MIX[p, rr, :] = (jnp.where(upper, outs[1], outs[0]) * inv).astype(BF)
        return carry

    lax.fori_loop(0, 4, attend, 0)

    wc_wait(1)
    wf_wait(1)

    acc = nn(MIX[0], WO[0:LANES, :])
    for p in range(1, 4):
        acc = acc + nn(MIX[p], WO[p * LANES : (p + 1) * LANES, :])
    ACC[...] = acc

    step = total // 8
    gain0, gain1 = gain[0:1, :].astype(F32), gain[1:2, :].astype(F32)
    shift0, shift1 = shift[0:1, :].astype(F32), shift[1:2, :].astype(F32)
    ob0, ob1 = obias[0:1, :].astype(F32), obias[1:2, :].astype(F32)

    def norm_one(i, carry):
        rr = aligned(i, step)
        res = X[rr, :].astype(F32) + off + (ACC[rr, :] + ob0)
        cen = res - jnp.mean(res, axis=-1, keepdims=True)
        fac = lax.rsqrt(jnp.mean(cen * cen, axis=-1, keepdims=True) + EPSILON)
        nrm = cen * fac
        N1[rr, :] = nrm
        LIVE[rr, 1:2] = fac
        HL[rr, :] = (nrm * gain0 + shift0).astype(BF)
        return carry

    lax.fori_loop(0, 8, norm_one, 0)

    ACC[...] = jnp.zeros_like(ACC)

    def ffn(k, carry):
        t = flip(tp, k)

        @pl.when(k == 1)
        def _():
            wc_wait(2)
            wc_wait(3)

        @pl.when(k == 2)
        def _():
            wf_start(2)
            wf_start(3)

        @pl.when(k == 3)
        def _():
            wf_wait(2)
            wf_wait(3)

        for c in range(2):
            rr = pl.ds(c * half, half)
            upper_bias = jnp.concatenate([SB[t, 2 + i : 3 + i, :] for i in range(4)], axis=1)
            u = nn(HL[rr, :], WU[t]) + upper_bias
            sq = u * u
            th = jnp.tanh(u * (GELU_C + (GELU_C * 0.044715) * sq))
            hp = 0.5 + 0.5 * th
            act = (u * hp).astype(BF)
            ACT2[t, rr, :] = act
            GP[t, rr, :] = (
                hp + (0.5 * u) * (1.0 - th * th) * (GELU_C + (3.0 * GELU_C * 0.044715) * sq)
            ).astype(BF)
            ACC[rr, :] += nn(act, WD[t])
        return carry

    lax.fori_loop(0, 4, ffn, 0)

    for k in (1, 2, 3):
        rows_wait(COT, s_c, r_c, k)

    SM[...] = jnp.zeros_like(SM)

    def norm_two(i, carry):
        rr = aligned(i, step)
        hid = N1[rr, :] * gain0 + shift0
        res = hid + (ACC[rr, :] + ob1)
        cen = res - jnp.mean(res, axis=-1, keepdims=True)
        fac = lax.rsqrt(jnp.mean(cen * cen, axis=-1, keepdims=True) + EPSILON)
        nrm = cen * fac
        live = LIVE[rr, 0:1]
        gf = COT[rr, :].astype(F32) * live
        COT[rr, :] = ((nrm * gain1 + shift1) * live).astype(BF)
        gn = gf * gain1
        g2 = fac * (
            gn - jnp.mean(gn, axis=-1, keepdims=True) - nrm * jnp.mean(gn * nrm, axis=-1, keepdims=True)
        )
        ACC[rr, :] = g2
        G2L[rr, :] = g2.astype(BF)
        SM[5:6, :] += jnp.sum(gf * nrm, axis=0, keepdims=True)
        SM[7:8, :] += jnp.sum(gf, axis=0, keepdims=True)
        SM[9:10, :] += jnp.sum(g2, axis=0, keepdims=True)
        return carry

    lax.fori_loop(0, 8, norm_two, 0)

    def back_copy(buf, dst, ss, rs, k):
        return rcopy(buf.at[aligned(flip(tp, k), rows), :], dst.at[tp], ss.at[k], rs.at[k], tp_peer(k))

    def back_wait(buf, dst, ss, rs, k):
        there = dst.at[flip(tp, k)]
        rcopy(buf.at[aligned(tp, rows), :], there, ss.at[k], rs.at[k], tp_peer(k)).wait_recv()

    outs_sent = [back_copy(COT, out_rows, s_out, r_out, k) for k in (2, 3, 1)]
    for copy in outs_sent:
        copy.start()
    out_local = pltpu.make_async_copy(COT.at[aligned(tp, rows), :], out_rows.at[tp], s_loc.at[0])
    out_local.start()

    def gref(m, t):
        return WU.at[t] if m == 2 else G.at[m, t]

    def core_send(m, j):
        k = 1 if j == 0 else 3
        return rcopy(gref(m, flip(tp, k)), RC.at[m, j], s_rc.at[m, j], r_rc.at[m, j], tp_peer(1))

    def core_wait(m, j):
        rcopy(RC.at[m, j], RC.at[m, j], s_rc.at[m, j], r_rc.at[m, j], tp_peer(1)).wait_recv()

    def x_send(m):
        return rcopy(gref(m, flip(tp, 2)), RX.at[m], s_rx.at[m], r_rx.at[m], tp_peer(2))

    def reduce_early(m, k):
        @pl.when(k == 0)
        def _():
            core_send(m, 1).start()

        @pl.when(k == 1)
        def _():
            core_wait(m, 1)
            t = flip(tp, 2)
            ref = gref(m, t)
            ref[...] = (ref[...].astype(F32) + RC[m, 1].astype(F32)).astype(BF)
            x_send(m).start()

        @pl.when(k == 2)
        def _():
            core_send(m, 0).start()

    qrows = 512 // quad

    def quad_send(m, j):
        return rcopy(
            gref(m, tp).at[aligned(quad_at(j), qrows), :], RQ.at[m, j - 1], s_rq.at[m, j - 1], r_rq.at[m, j - 1],
            quad_peer(j),
        )

    def rest_send(m, j):
        return rcopy(RE.at[m, r_id], RE.at[m, r_id], s_re.at[m, j - 1], r_re.at[m, j - 1], rest_peer(j))

    def rest_wait(m, j):
        there = RE.at[m, lax.rem(r_id + rest_n - j, rest_n)]
        rcopy(there, there, s_re.at[m, j - 1], r_re.at[m, j - 1], rest_peer(j)).wait_recv()

    def ag_send(m, j):
        here = RX.at[m, aligned(q_id, qrows), :]
        return rcopy(here, here, s_ag.at[m, j - 1], r_ag.at[m, j - 1], quad_peer(j))

    def ag_wait(m, j):
        there = RX.at[m, aligned(quad_at(-j), qrows), :]
        rcopy(there, there, s_ag.at[m, j - 1], r_ag.at[m, j - 1], quad_peer(j)).wait_recv()

    def reduce_quad(m):
        core_wait(m, 0)
        rcopy(RX.at[m], RX.at[m], s_rx.at[m], r_rx.at[m], tp_peer(2)).wait_recv()
        ref = gref(m, tp)
        ref[...] = (ref[...].astype(F32) + RC[m, 0].astype(F32) + RX[m].astype(F32)).astype(BF)
        for j in range(1, quad):
            quad_send(m, j).start()

    def reduce_rest(m):
        for j in range(1, quad):
            quad_send(m, j).wait_recv()
        acc_q = gref(m, tp)[aligned(q_id, qrows), :].astype(F32)
        for j in range(quad - 1):
            acc_q = acc_q + RQ[m, j].astype(F32)
        RE[m, r_id] = acc_q.astype(BF)
        for j in range(1, rest_n):
            rest_send(m, j).start()

    def reduce_gather(m):
        for j in range(1, rest_n):
            rest_wait(m, j)
        acc_r = RE[m, 0].astype(F32)
        for j in range(1, rest_n):
            acc_r = acc_r + RE[m, j].astype(F32)
        RX[m, aligned(q_id, qrows), :] = acc_r.astype(BF)
        for j in range(1, quad):
            ag_send(m, j).start()

    def reduce_done(m):
        for j in range(1, quad):
            ag_wait(m, j)


    def ffn_back(k, carry):
        t = flip(tp, 3 - k)
        d_act = nt(G2L[...], WD[t])
        g_pre = d_act * GP[t].astype(F32)
        SM[pl.ds(10 + t, 1), :] = jnp.sum(g_pre, axis=0, keepdims=True)
        low = g_pre.astype(BF)
        GP[t] = low
        G[0, t] = tn(ACT2[t], G2L[...]).astype(BF)
        G[1, t] = tn(HL[...], low).astype(BF)
        ACC[...] += nt(low, WU[t])
        reduce_early(0, k)
        reduce_early(1, k)
        return carry

    lax.fori_loop(0, 4, ffn_back, 0)

    def norm_one_back(i, carry):
        rr = aligned(i, step)
        gh = ACC[rr, :]
        nrm = N1[rr, :]
        gn = gh * gain0
        g1 = LIVE[rr, 1:2] * (
            gn - jnp.mean(gn, axis=-1, keepdims=True) - nrm * jnp.mean(gn * nrm, axis=-1, keepdims=True)
        )
        ACC[rr, :] = g1
        G2L[rr, :] = g1.astype(BF)
        SM[4:5, :] += jnp.sum(gh * nrm, axis=0, keepdims=True)
        SM[6:7, :] += jnp.sum(gh, axis=0, keepdims=True)
        SM[8:9, :] += jnp.sum(g1, axis=0, keepdims=True)
        return carry

    lax.fori_loop(0, 8, norm_one_back, 0)

    def back_prep(p, carry):
        gm = nt(G2L[...], WO[aligned(p, LANES), :])
        WU[p, pl.ds(3 * LANES, LANES), :] = tn(MIX[p], G2L[...]).astype(BF)
        lane_f = lax.broadcasted_iota(jnp.int32, (total, LANES), 1)
        up_f = lane_f >= HD
        gs = gm * LINV[p]
        prod = gs * MIX[p].astype(F32)
        low = gs.astype(BF)
        for e in range(2):
            mine = up_f if e == 1 else jnp.logical_not(up_f)
            delta = jnp.sum(jnp.where(mine, prod, 0.0), axis=-1, keepdims=True)
            hi = delta.astype(BF)
            lo = (delta - hi.astype(F32)).astype(BF)
            base = HD * (1 - e)
            side = jnp.where(lane_f == base, hi, jnp.where(lane_f == base + 1, lo, zero))
            GP[p, :, pl.ds(e * LANES, LANES)] = jnp.where(mine, low, side)
        return carry

    wf_send(2).wait_send()
    for j in range(1, quad):
        wq_send(2, j).wait_send()
    lax.fori_loop(0, 4, back_prep, 0)

    ones = jnp.ones((8, total), BF)
    lane_f = lax.broadcasted_iota(jnp.int32, (total, LANES), 1)
    up_f = lane_f >= HD

    def attend_back(k, carry):
        p = flip(tp, 3 - k)
        d_k, d_v = [], []
        for c in range(2):
            rr = pl.ds(c * half, half)
            part = []
            for e in range(2):
                h = 2 * p + e
                go = GP[p, rr, pl.ds(e * LANES, LANES)]
                prob = PR[h, rr, :]
                d_s = (prob.astype(F32) * nt(go, VA[h])).astype(BF)
                part.append(nn(d_s, KA[h]))
                more = (tn(prob, go), tn(d_s, QA[h, rr, :]))
                if c == 0:
                    d_v.append(more[0])
                    d_k.append(more[1])
                else:
                    d_v[e] = d_v[e] + more[0]
                    d_k[e] = d_k[e] + more[1]
            ACT2[p, rr, 0:LANES] = (jnp.where(upper, part[1], part[0]) * 0.125).astype(BF)
        ACT2[p, :, LANES : 2 * LANES] = jnp.where(up_f, d_k[1], d_k[0]).astype(BF)
        ACT2[p, :, 2 * LANES : 3 * LANES] = jnp.where(up_f, d_v[1], d_v[0]).astype(BF)
        d_all = ACT2[p, :, 0 : 3 * LANES]
        WU[p, 0 : 3 * LANES, :] = tn(d_all, ACT[...]).astype(BF)
        sums = nn(ones, d_all)
        SM[14:15, aligned(p, LANES)] = sums[0:1, 0:LANES]
        SM[15:16, aligned(p, LANES)] = sums[0:1, 2 * LANES : 3 * LANES]
        reduce_early(2, k)

        @pl.when(k == 1)
        def _():
            reduce_quad(0)

        @pl.when(k == 2)
        def _():
            reduce_quad(1)

        @pl.when(k == 3)
        def _():
            reduce_rest(0)

        return carry

    lax.fori_loop(0, 4, attend_back, 0)

    reduce_quad(2)
    reduce_rest(1)
    reduce_gather(0)

    def input_grad(k, carry):
        b = flip(tp, 3 - k)
        rr = aligned(b, rows)
        grad = ACC[rr, :]
        for p in range(4):
            grad = grad + nt(ACT2[p, rr, 0 : 3 * LANES], WP[p])
        X[rr, :] = grad.astype(BF)
        SM[0:1, :] += jnp.sum(grad, axis=0, keepdims=True)

        @pl.when(k < 3)
        def _():
            kk = 3 - k
            rcopy(X.at[rr, :], ig_rows.at[tp], s_ig.at[kk], r_ig.at[kk], (dp, b)).start()

        return carry

    lax.fori_loop(0, 4, input_grad, 0)
    ig_local = pltpu.make_async_copy(X.at[aligned(tp, rows), :], ig_rows.at[tp], s_loc.at[1])
    ig_local.start()

    base_sum = SM[0:1, :]
    for c in range(dbias.shape[0]):
        SM[c : c + 1, :] = jnp.where(ds_here == c, 1.0, 0.0) * base_sum

    def sm_all(src, slots, me, count, sem0, peer_of, from_of):
        slots[me] = src
        copies = []
        for j in range(1, count):
            copies.append(rcopy(slots.at[me], slots.at[me], s_sm.at[sem0 + j], r_sm.at[sem0 + j], peer_of(j)))
        for copy in copies:
            copy.start()
        for j in range(1, count):
            there = slots.at[from_of(j)]
            rcopy(there, there, s_sm.at[sem0 + j], r_sm.at[sem0 + j], peer_of(j)).wait_recv()
        out = slots[0]
        for j in range(1, count):
            out = out + slots[j]
        return out, copies

    reduce_rest(2)
    reduce_gather(1)
    val, c1 = sm_all(SM[...], SMT, tp, 4, 0, tp_peer, lambda j: flip(tp, j))
    val, c2 = sm_all(val, SMQ, q_id, quad, 4, quad_peer, lambda j: quad_at(-j))
    reduce_gather(2)
    val, c3 = sm_all(val, SMR, r_id, rest_n, 4 + quad, rest_peer, lambda j: lax.rem(r_id + rest_n - j, rest_n))
    g_small[...] = val

    for m in range(3):
        reduce_done(m)
    result = pltpu.make_async_copy(RX, g_sum, s_res)
    result.start()

    for k in (1, 2, 3):
        back_wait(COT, out_rows, s_out, r_out, k)
        back_wait(X, ig_rows, s_ig, r_ig, k)
        back_copy(X, ig_rows, s_ig, r_ig, k).wait_send()
    ig_local.wait()
    out_local.wait()
    result.wait()
    for copy in sends + outs_sent + c1 + c2 + c3:
        copy.wait_send()
    for g in (0, 1, 3):
        wf_send(g).wait_send()
        for j in range(1, quad):
            wq_send(g, j).wait_send()
    for m in range(3):
        core_send(m, 0).wait_send()
        core_send(m, 1).wait_send()
        x_send(m).wait_send()
        for j in range(1, quad):
            quad_send(m, j).wait_send()
            ag_send(m, j).wait_send()
        for j in range(1, rest_n):
            rest_send(m, j).wait_send()


def finish(
    raw_out, raw_ig, g_sum, g_small,
    out_rows, ig_rows, g_qkv, g_out, g_up, g_down, g_dbias, g_gain, g_shift, g_obias, g_upb, g_qvb,
):
    i = pl.program_id(0)
    tp = lax.axis_index("tp")
    out_rows[...] = raw_out[...]
    ig_rows[...] = raw_ig[...]
    g_down[...] = g_sum[0].astype(F32)
    g_up[...] = g_sum[1].astype(F32)

    @pl.when(i < 3)
    def _():
        g_qkv[0] = jnp.transpose(g_sum[2].astype(F32))

    @pl.when(i == 3)
    def _():
        g_out[...] = g_sum[2].astype(F32)

    @pl.when(i == 0)
    def _():
        g_dbias[...] = g_small[0:4, :]
        g_gain[...] = g_small[4:6, :]
        g_shift[...] = g_small[6:8, :]
        g_obias[...] = g_small[8:10, :]
        g_upb[...] = g_small[pl.ds(10 + tp, 1), :]
        g_qvb[...] = g_small[14:16, aligned(tp, LANES)]


def shards(dp_n, *args):
    (inputs, dataset, variate_mask, dataset_bias, w_qkv, qv_bias, w_out, out_bias, w_up, up_bias, w_down,
     norm_gain, norm_shift, cotangent) = args
    win, rows, width = inputs.shape
    total = variate_mask.shape[1]
    quad = 4 if dp_n <= 16 else 8
    rest_n = dp_n // quad
    ffs = w_up.shape[1]
    assert win == 4 and total == 4 * rows and width == 512 and ffs == 512 and w_out.shape[0] == LANES
    any_spec = pl.BlockSpec(memory_space=pl.ANY)
    vmem = pl.BlockSpec(memory_space=pltpu.VMEM)
    smem = pl.BlockSpec(memory_space=pltpu.SMEM)
    dma = pltpu.SemaphoreType.DMA
    V = pltpu.VMEM
    scratch = [
        V((total, width), BF),
        V((total, width), BF),
        V((4, width, 3 * LANES), BF),
        V((width, width), BF),
        V((4, width, ffs), BF),
        V((4, ffs, width), BF),
        V((4, 8, LANES), F32),
        V((total, width), BF),
        V((8, total, LANES), BF),
        V((8, total, LANES), BF),
        V((8, total, LANES), BF),
        V((8, total, total), BF),
        V((4, total, LANES), BF),
        V((4, total, LANES), F32),
        V((total, width), F32),
        V((total, width), BF),
        V((4, total, ffs), BF),
        V((4, total, ffs), BF),
        V((total, width), F32),
        V((total, width), BF),
        V((total, LANES), F32),
        V((2, 4, width, ffs), BF),
        V((3, 2, width, ffs), BF),
        V((3, width, ffs), BF),
        V((3, quad - 1, width // quad, ffs), BF),
        V((3, rest_n, width // quad, ffs), BF),
        V((16, width), F32),
        V((4, 16, width), F32),
        V((quad, 16, width), F32),
        V((rest_n, 16, width), F32),
        dma((8,)),
        dma((4,)), dma((4,)),
        dma((4,)), dma((4,)),
        dma((6,)), dma((6,)),
        dma((4, quad - 1)), dma((4, quad - 1)),
        dma((4,)), dma((4,)),
        dma((6,)), dma((6,)),
        dma((4,)), dma((4,)),
        dma((4,)), dma((4,)),
        dma((4,)), dma((4,)),
        dma((2,)),
        dma((3, 2)), dma((3, 2)),
        dma((3,)), dma((3,)),
        dma((3, quad - 1)), dma((3, quad - 1)),
        dma((3, max(rest_n - 1, 1))), dma((3, max(rest_n - 1, 1))),
        dma((3, quad - 1)), dma((3, quad - 1)),
        dma((4 + quad + rest_n,)), dma((4 + quad + rest_n,)),
        dma,
    ]
    sds = jax.ShapeDtypeStruct
    outs = pl.pallas_call(
        functools.partial(kernel, quad, rest_n),
        out_shape=(
            sds((win, rows, width), BF),
            sds((win, rows, width), BF),
            sds((3, width, ffs), BF),
            sds((16, width), F32),
        ),
        in_specs=[any_spec, any_spec, smem, vmem, vmem, any_spec, vmem, any_spec, vmem, any_spec, vmem, any_spec, vmem, vmem],
        out_specs=(any_spec,) * 3 + (vmem,),
        scratch_shapes=scratch,
        compiler_params=pltpu.CompilerParams(
            collective_id=0, has_side_effects=True, vmem_limit_bytes=65000000
        ),
        cost_estimate=pl.CostEstimate(flops=30 * 10**9, bytes_accessed=20 * 10**6, transcendentals=10**7),
        name="encoder_layer",
    )(inputs, cotangent, dataset, variate_mask, dataset_bias, w_qkv, qv_bias, w_out, out_bias, w_up,
      up_bias.reshape(4, LANES), w_down, norm_gain, norm_shift)
    raw_out, raw_ig, g_sum, g_small = outs
    res = pl.pallas_call(
        finish,
        out_shape=(
            sds((win, rows, width), BF),
            sds((win, rows, width), BF),
            sds((3, width, LANES), F32),
            sds((LANES, width), F32),
            sds((width, ffs), F32),
            sds((ffs, width), F32),
            sds((4, width), F32),
            sds((2, width), F32),
            sds((2, width), F32),
            sds((2, width), F32),
            sds((1, width), F32),
            sds((2, LANES), F32),
        ),
        grid=(4,),
        in_specs=[
            pl.BlockSpec((1, rows, width), lambda i: (i, 0, 0)),
            pl.BlockSpec((1, rows, width), lambda i: (i, 0, 0)),
            pl.BlockSpec((3, LANES, ffs), lambda i: (0, i, 0)),
            pl.BlockSpec((16, width), lambda i: (0, 0)),
        ],
        out_specs=(
            pl.BlockSpec((1, rows, width), lambda i: (i, 0, 0)),
            pl.BlockSpec((1, rows, width), lambda i: (i, 0, 0)),
            pl.BlockSpec((1, width, LANES), lambda i: (jnp.minimum(i, 2), 0, 0)),
            pl.BlockSpec((LANES, width), lambda i: (0, 0)),
            pl.BlockSpec((LANES, ffs), lambda i: (i, 0)),
            pl.BlockSpec((LANES, width), lambda i: (i, 0)),
            pl.BlockSpec((4, width), lambda i: (0, 0)),
            pl.BlockSpec((2, width), lambda i: (0, 0)),
            pl.BlockSpec((2, width), lambda i: (0, 0)),
            pl.BlockSpec((2, width), lambda i: (0, 0)),
            pl.BlockSpec((1, width), lambda i: (0, 0)),
            pl.BlockSpec((2, LANES), lambda i: (0, 0)),
        ),
        name="write_results",
    )(raw_out, raw_ig, g_sum, g_small)
    (rows_out, rows_ig, g_qkv, g_out, g_up, g_down, g_dbias, g_gain, g_shift, g_obias, g_upb, g_qvb) = res
    return (
        rows_out, rows_ig, g_dbias, g_qkv, g_qvb, g_out, g_obias, g_up, g_upb.reshape(-1), g_down, g_gain, g_shift,
    )


def solution(mesh):
    in_specs = (
        P("dp", "tp", None), P("dp"), P("dp", None), P(), P(None, None, "tp"), P(None, "tp"), P("tp", None), P(),
        P(None, "tp"), P("tp"), P("tp", None), P(), P(), P("dp", "tp", None),
    )
    out_specs = (
        P("dp", "tp", None), P("dp", "tp", None), P(), P(None, None, "tp"), P(None, "tp"), P("tp", None), P(),
        P(None, "tp"), P("tp"), P("tp", None), P(), P(),
    )
    body = functools.partial(shards, mesh.shape["dp"])
    return jax.shard_map(body, mesh=mesh, in_specs=in_specs, out_specs=out_specs, check_vma=False)
```

```python
import functools
import math

import jax
import jax.numpy as jnp
from jax import lax
from jax.experimental import pallas as pl
from jax.experimental.pallas import tpu as pltpu
from jax.sharding import PartitionSpec as P

HD = 64
EPSILON = 1e-05
NEG_FILL = -1e30
BF = jnp.bfloat16
F32 = jnp.float32
MESH = pl.DeviceIdType.MESH
GELU_C = math.sqrt(2.0 / math.pi)
LANES = 128


def nn(a, b):
    return jnp.dot(a, b, preferred_element_type=F32)


def nt(a, b):
    return lax.dot_general(a, b, (((1,), (1,)), ((), ())), preferred_element_type=F32)


def tn(a, b):
    return lax.dot_general(a, b, (((0,), (0,)), ((), ())), preferred_element_type=F32)


def flip(value, k):
    low = lax.rem(lax.rem(value, 2) + k % 2, 2) if isinstance(k, int) else lax.rem(lax.rem(value, 2) + lax.rem(k, 2), 2)
    high = lax.rem(lax.div(value, 2) + (k // 2 if isinstance(k, int) else lax.div(k, 2)), 2)
    return high * 2 + low


def aligned(index, size):
    return pl.ds(pl.multiple_of(index * size, size), size)


def kernel(
    quad, rest_n,
    x_in, cot_in, dataset, mask, dbias, w_qkv, qvb, w_out, obias, w_up, upb, w_down, gain, shift,
    out_rows, ig_rows, g_sum, g_small,
    X, COT, WP, WO, WU, WD, SB, ACT, QA, KA, VA, PR, MIX, LINV, N1, HL, ACT2, GP, ACC, G2L, LIVE,
    G, RC, RX, RQ, RB, RE, SD, SM, SMT, SMQ, SMR,
    s_own, s_x, r_x, s_c, r_c, s_wx, r_wx, s_wq, r_wq, s_wf, r_wf, s_wc, r_wc, s_b, r_b, s_out, r_out, s_ig, r_ig, s_loc,
    s_rc, r_rc, s_rx, r_rx, s_rq, r_rq, s_rb, r_rb, s_re, r_re, s_ag, r_ag, s_sm, r_sm, s_res,
):
    dp = lax.axis_index("dp")
    tp = lax.axis_index("tp")
    q_id = lax.rem(dp, quad)
    r_id = lax.div(dp, quad)
    rows = x_in.shape[1]
    total, width = X.shape
    half = total // 2
    x_id = lax.div(tp, 2)

    def tp_peer(k):
        return (dp, flip(tp, k))

    def quad_at(j):
        return lax.rem(q_id + j + quad, quad)

    def quad_peer(j):
        return (r_id * quad + quad_at(j), tp)

    def rest_peer(j):
        return (lax.rem(r_id + j, rest_n) * quad + q_id, tp)

    def rcopy(src, dst, ss, rs, dev):
        return pltpu.make_async_remote_copy(
            src_ref=src, dst_ref=dst, send_sem=ss, recv_sem=rs, device_id=dev, device_id_type=MESH
        )

    barrier = pltpu.get_barrier_semaphore()
    peers = [tp_peer(k) for k in (1, 2, 3)] + [quad_peer(j) for j in range(1, quad)]
    peers += [rest_peer(j) for j in range(1, rest_n)]
    for peer in peers:
        pl.semaphore_signal(barrier, inc=1, device_id=peer, device_id_type=MESH)

    own = [pltpu.make_async_copy(x_in.at[tp], X.at[aligned(tp, rows), :], s_own.at[0])]
    for i in range(3):
        own.append(pltpu.make_async_copy(w_qkv.at[i], WP.at[tp, :, pl.ds(i * LANES, LANES)], s_own.at[1 + i]))
    own.append(pltpu.make_async_copy(w_out, WO.at[aligned(tp, LANES), :], s_own.at[4]))
    own.append(pltpu.make_async_copy(w_up, WU.at[tp], s_own.at[5]))
    own.append(pltpu.make_async_copy(w_down, WD.at[tp], s_own.at[6]))
    own.append(pltpu.make_async_copy(cot_in.at[tp], COT.at[aligned(tp, rows), :], s_own.at[7]))
    for copy in own:
        copy.start()

    SB[tp, 0:2, :] = qvb[...].astype(F32)
    SB[tp, 2:6, :] = upb[...].astype(F32)
    pl.semaphore_wait(barrier, len(peers))

    wq = width // quad
    oq = LANES // quad

    def w_whole(g, t):
        return (WP.at[t], WO.at[aligned(t, LANES), :], WU.at[t], WD.at[t])[g]

    def w_part(g, t, q):
        if g == 1:
            return WO.at[pl.ds(pl.multiple_of(t * LANES + q * oq, oq), oq), :]
        return (WP, WO, WU, WD)[g].at[t, aligned(q, wq), :]

    def wx_dst(i, t):
        if i < 3:
            return WP.at[t, aligned(q_id, wq), pl.ds(i * LANES, LANES)]
        return w_part(i - 2, t, q_id)

    wx_src = [w_qkv.at[i, aligned(q_id, wq), :] for i in range(3)]
    wx_src += [w_out.at[aligned(q_id, oq), :], w_up.at[aligned(q_id, wq), :], w_down.at[aligned(q_id, wq), :]]
    members = {0: (0, 1, 2), 1: (3,), 2: (4,), 3: (5,)}

    def wx_send(i):
        return rcopy(wx_src[i], wx_dst(i, tp), s_wx.at[i], r_wx.at[i], tp_peer(2))

    def wx_wait(g):
        for i in members[g]:
            there = wx_dst(i, flip(tp, 2))
            rcopy(there, there, s_wx.at[i], r_wx.at[i], tp_peer(2)).wait_recv()

    def wq_send(g, j):
        here = w_part(g, flip(tp, 2), q_id)
        return rcopy(here, here, s_wq.at[g, j - 1], r_wq.at[g, j - 1], quad_peer(j))

    def wq_start(g):
        wx_wait(g)
        for j in range(1, quad):
            wq_send(g, j).start()

    def wf_send(g):
        here = w_whole(g, flip(tp, 2))
        return rcopy(here, here, s_wf.at[g], r_wf.at[g], tp_peer(1))

    def wf_start(g):
        for j in range(1, quad):
            there = w_part(g, flip(tp, 2), quad_at(-j))
            rcopy(there, there, s_wq.at[g, j - 1], r_wq.at[g, j - 1], quad_peer(j)).wait_recv()
        wf_send(g).start()

    def wf_wait(g):
        there = w_whole(g, flip(tp, 3))
        rcopy(there, there, s_wf.at[g], r_wf.at[g], tp_peer(1)).wait_recv()

    def wc_dst(i, t):
        return WP.at[t, :, pl.ds(i * LANES, LANES)] if i < 3 else w_whole(i - 2, t)

    wc_src = [w_qkv.at[0], w_qkv.at[1], w_qkv.at[2], w_out, w_up, w_down]

    def wc_send(i):
        return rcopy(wc_src[i], wc_dst(i, tp), s_wc.at[i], r_wc.at[i], tp_peer(1))

    def wc_wait(g):
        for i in members[g]:
            there = wc_dst(i, flip(tp, 1))
            rcopy(there, there, s_wc.at[i], r_wc.at[i], tp_peer(1)).wait_recv()

    def rows_copy(src, dst, ss, rs, k):
        return rcopy(src.at[flip(tp, k)], dst.at[aligned(tp, rows), :], ss.at[k], rs.at[k], tp_peer(k))

    def rows_wait(dst, ss, rs, k):
        there = dst.at[aligned(flip(tp, k), rows), :]
        rcopy(there, there, ss.at[k], rs.at[k], tp_peer(k)).wait_recv()

    def sb_copy(k):
        return rcopy(SB.at[tp], SB.at[tp], s_b.at[k], r_b.at[k], tp_peer(k))

    sends = []
    for k in (1, 2, 3):
        sends.append(sb_copy(k))
    for i in range(4):
        sends.append(wx_send(i))
    for i in range(4):
        sends.append(wc_send(i))
    for k in (2, 3, 1):
        sends.append(rows_copy(x_in, X, s_x, r_x, k))
    for i in (4, 5):
        sends.append(wx_send(i))
        sends.append(wc_send(i))
    for k in (2, 3, 1):
        sends.append(rows_copy(cot_in, COT, s_c, r_c, k))
    for copy in sends:
        copy.start()

    live_row = mask[pl.ds(tp, 1), :].astype(F32)
    LIVE[:, 0:8] = jnp.transpose(jnp.broadcast_to(live_row, (8, total)))
    ds_here = dataset[tp]
    off = jnp.zeros((1, X.shape[1]), F32)
    for c in range(dbias.shape[0]):
        off = off + jnp.where(ds_here == c, 1.0, 0.0) * dbias[c : c + 1, :].astype(F32)

    for copy in own:
        copy.wait()
    for k in (1, 2, 3):
        there = SB.at[flip(tp, k)]
        rcopy(there, there, s_b.at[k], r_b.at[k], tp_peer(k)).wait_recv()

    lane = lax.broadcasted_iota(jnp.int32, (half, LANES), 1)
    upper = lane >= HD
    one = jnp.ones((), BF)
    zero = jnp.zeros((), BF)

    def project(hh, first):
        rr = aligned(hh, half)
        ACT[rr, :] = (X[rr, :].astype(F32) + off).astype(BF)
        fill = jnp.where(LIVE[rr, 0:1] > 0.5, 0.0, NEG_FILL).astype(BF)
        fill = jnp.broadcast_to(fill, (half, LANES))

        def shard(k, carry):
            t = flip(tp, k)
            if first:
                @pl.when(k == 1)
                def _():
                    wc_wait(0)

                @pl.when(k == 2)
                def _():
                    wf_start(0)
                    wf_start(1)

                @pl.when(k == 3)
                def _():
                    wf_wait(0)

            qkv = nn(ACT[rr, :], WP[t])
            query = (qkv[:, :LANES] + SB[t, 0:1, :]).astype(BF) * BF(0.125)
            keys = qkv[:, LANES : 2 * LANES].astype(BF)
            vals = (qkv[:, 2 * LANES :] + SB[t, 1:2, :]).astype(BF)
            QA[2 * t, rr, :] = jnp.where(upper, jnp.where(lane == HD, one, zero), query)
            QA[2 * t + 1, rr, :] = jnp.where(upper, query, jnp.where(lane == 0, one, zero))
            KA[2 * t, rr, :] = jnp.where(upper, jnp.where(lane == HD, fill, zero), keys)
            KA[2 * t + 1, rr, :] = jnp.where(upper, keys, jnp.where(lane == 0, fill, zero))
            VA[2 * t, rr, :] = jnp.where(upper, -one, vals)
            VA[2 * t + 1, rr, :] = jnp.where(upper, vals, -one)
            return carry

        lax.fori_loop(0, 4, shard, 0)

    wq_start(0)
    wq_start(1)
    rows_wait(X, s_x, r_x, 1)
    project(x_id, True)
    rows_wait(X, s_x, r_x, 2)
    rows_wait(X, s_x, r_x, 3)
    project(1 - x_id, False)

    def attend(p, carry):
        @pl.when(p == 2)
        def _():
            wq_start(2)
            wq_start(3)

        for c in range(2):
            rr = pl.ds(c * half, half)
            outs = []
            for e in range(2):
                h = 2 * p + e
                scores = nt(QA[h, rr, :], KA[h])
                top = jnp.max(scores, axis=1, keepdims=True)
                weight = jnp.exp(scores - top).astype(BF)
                PR[h, rr, :] = weight
                outs.append(nn(weight, VA[h]))
            inv = -1.0 / jnp.where(upper, pltpu.roll(outs[1], HD, 1), pltpu.roll(outs[0], HD, 1))
            LINV[p, rr, :] = inv
            MIX[p, rr, :] = (jnp.where(upper, outs[1], outs[0]) * inv).astype(BF)
        return carry

    lax.fori_loop(0, 4, attend, 0)

    wc_wait(1)
    wf_wait(1)

    acc = nn(MIX[0], WO[0:LANES, :])
    for p in range(1, 4):
        acc = acc + nn(MIX[p], WO[p * LANES : (p + 1) * LANES, :])
    ACC[...] = acc

    step = total // 8
    gain0, gain1 = gain[0:1, :].astype(F32), gain[1:2, :].astype(F32)
    shift0, shift1 = shift[0:1, :].astype(F32), shift[1:2, :].astype(F32)
    ob0, ob1 = obias[0:1, :].astype(F32), obias[1:2, :].astype(F32)

    def norm_one(i, carry):
        rr = aligned(i, step)
        res = X[rr, :].astype(F32) + off + (ACC[rr, :] + ob0)
        cen = res - jnp.mean(res, axis=-1, keepdims=True)
        fac = lax.rsqrt(jnp.mean(cen * cen, axis=-1, keepdims=True) + EPSILON)
        nrm = cen * fac
        N1[rr, :] = nrm
        LIVE[rr, 1:2] = fac
        HL[rr, :] = (nrm * gain0 + shift0).astype(BF)
        return carry

    lax.fori_loop(0, 8, norm_one, 0)

    ACC[...] = jnp.zeros_like(ACC)

    def ffn(k, carry):
        t = flip(tp, k)

        @pl.when(k == 1)
        def _():
            wc_wait(2)
            wc_wait(3)

        @pl.when(k == 2)
        def _():
            wf_start(2)
            wf_start(3)

        @pl.when(k == 3)
        def _():
            wf_wait(2)
            wf_wait(3)

        for c in range(2):
            rr = pl.ds(c * half, half)
            upper_bias = jnp.concatenate([SB[t, 2 + i : 3 + i, :] for i in range(4)], axis=1)
            u = nn(HL[rr, :], WU[t]) + upper_bias
            sq = u * u
            th = jnp.tanh(u * (GELU_C + (GELU_C * 0.044715) * sq))
            hp = 0.5 + 0.5 * th
            act = (u * hp).astype(BF)
            ACT2[t, rr, :] = act
            GP[t, rr, :] = (
                hp + (0.5 * u) * (1.0 - th * th) * (GELU_C + (3.0 * GELU_C * 0.044715) * sq)
            ).astype(BF)
            ACC[rr, :] += nn(act, WD[t])
        return carry

    lax.fori_loop(0, 4, ffn, 0)

    for k in (1, 2, 3):
        rows_wait(COT, s_c, r_c, k)

    SM[...] = jnp.zeros_like(SM)

    def norm_two(i, carry):
        rr = aligned(i, step)
        hid = N1[rr, :] * gain0 + shift0
        res = hid + (ACC[rr, :] + ob1)
        cen = res - jnp.mean(res, axis=-1, keepdims=True)
        fac = lax.rsqrt(jnp.mean(cen * cen, axis=-1, keepdims=True) + EPSILON)
        nrm = cen * fac
        live = LIVE[rr, 0:1]
        gf = COT[rr, :].astype(F32) * live
        COT[rr, :] = ((nrm * gain1 + shift1) * live).astype(BF)
        gn = gf * gain1
        g2 = fac * (
            gn - jnp.mean(gn, axis=-1, keepdims=True) - nrm * jnp.mean(gn * nrm, axis=-1, keepdims=True)
        )
        ACC[rr, :] = g2
        G2L[rr, :] = g2.astype(BF)
        SM[5:6, :] += jnp.sum(gf * nrm, axis=0, keepdims=True)
        SM[7:8, :] += jnp.sum(gf, axis=0, keepdims=True)
        SM[9:10, :] += jnp.sum(g2, axis=0, keepdims=True)
        return carry

    lax.fori_loop(0, 8, norm_two, 0)

    def back_copy(buf, dst, ss, rs, k):
        return rcopy(buf.at[aligned(flip(tp, k), rows), :], dst.at[tp], ss.at[k], rs.at[k], tp_peer(k))

    def back_wait(buf, dst, ss, rs, k):
        there = dst.at[flip(tp, k)]
        rcopy(buf.at[aligned(tp, rows), :], there, ss.at[k], rs.at[k], tp_peer(k)).wait_recv()

    outs_sent = [back_copy(COT, out_rows, s_out, r_out, k) for k in (2, 3, 1)]
    outs_sent[0].start()
    outs_sent[2].start()
    out_local = pltpu.make_async_copy(COT.at[aligned(tp, rows), :], out_rows.at[tp], s_loc.at[0])
    out_local.start()

    pieces = ((0, 0, width), (1, 0, width)) + tuple((2, g * LANES, LANES) for g in (3, 2, 1, 0))

    def gref(i, t):
        m, r0, n = pieces[i]
        return WU.at[t, pl.ds(r0, n), :] if m == 2 else G.at[m, t]

    def gchunk(i, t, q):
        m, r0, n = pieces[i]
        at = pl.ds(pl.multiple_of(r0 + q * (n // quad), 16), n // quad)
        return WU.at[t, at, :] if m == 2 else G.at[m, t, at, :]

    def rxchunk(i, q):
        m, r0, n = pieces[i]
        return RX.at[m, pl.ds(pl.multiple_of(r0 + q * (n // quad), 16), n // quad), :]

    def span(i):
        return pl.ds(pieces[i][1], pieces[i][2])

    def qspan(i):
        return pl.ds(pieces[i][1] // quad, pieces[i][2] // quad)

    def core_send(i, j):
        there = RC.at[pieces[i][0], j, span(i), :]
        return rcopy(gref(i, flip(tp, 1 if j == 0 else 3)), there, s_rc.at[i, j], r_rc.at[i, j], tp_peer(1))

    def core_add(i, j):
        there = RC.at[pieces[i][0], j, span(i), :]
        rcopy(there, there, s_rc.at[i, j], r_rc.at[i, j], tp_peer(1)).wait_recv()
        ref = gref(i, flip(tp, 2) if j == 1 else tp)
        ref[...] = (ref[...].astype(F32) + there[...].astype(F32)).astype(BF)

    def x_send(i):
        if i == 1:
            src, dst = gchunk(i, flip(tp, 2), q_id), rxchunk(i, q_id)
        else:
            src, dst = gref(i, flip(tp, 2)), RX.at[pieces[i][0], span(i), :]
        return rcopy(src, dst, s_rx.at[i], r_rx.at[i], tp_peer(2))

    def quad_send(i, j, other=False):
        if other:
            return rcopy(gchunk(i, flip(tp, 2), quad_at(j)), RB.at[j - 1], s_rb.at[j - 1], r_rb.at[j - 1], quad_peer(j))
        there = RQ.at[pieces[i][0], j - 1, qspan(i), :]
        return rcopy(gchunk(i, tp, quad_at(j)), there, s_rq.at[i, j - 1], r_rq.at[i, j - 1], quad_peer(j))

    def quad_start(i, other=False):
        for j in range(1, quad):
            quad_send(i, j, other).start()

    def rest_send(i, j):
        here = RE.at[pieces[i][0], r_id, qspan(i), :]
        return rcopy(here, here, s_re.at[i, j - 1], r_re.at[i, j - 1], rest_peer(j))

    def ag_send(i, j):
        here = rxchunk(i, q_id)
        return rcopy(here, here, s_ag.at[i, j - 1], r_ag.at[i, j - 1], quad_peer(j))

    def reduce_x(i):
        core_add(i, 1)
        x_send(i).start()

    def reduce_quad(i):
        core_add(i, 0)
        x_send(i).wait_recv()
        ref = gref(i, tp)
        ref[...] = (ref[...].astype(F32) + RX[pieces[i][0], span(i), :].astype(F32)).astype(BF)
        quad_start(i)

    def reduce_other(i):
        for j in range(1, quad):
            quad_send(i, j, True).wait_recv()
        ref = gchunk(i, flip(tp, 2), q_id)
        acc_q = ref[...].astype(F32)
        for j in range(quad - 1):
            acc_q = acc_q + RB[j].astype(F32)
        ref[...] = acc_q.astype(BF)
        x_send(i).start()

    def reduce_rest(i):
        m = pieces[i][0]
        for j in range(1, quad):
            quad_send(i, j).wait_recv()
        acc_q = gchunk(i, tp, q_id)[...].astype(F32)
        for j in range(quad - 1):
            acc_q = acc_q + RQ[m, j, qspan(i), :].astype(F32)
        if i == 1:
            x_send(i).wait_recv()
            acc_q = acc_q + rxchunk(i, q_id)[...].astype(F32)
        RE[m, r_id, qspan(i), :] = acc_q.astype(BF)
        for j in range(1, rest_n):
            rest_send(i, j).start()

    def reduce_gather(i):
        m = pieces[i][0]
        for j in range(1, rest_n):
            there = RE.at[m, lax.rem(r_id + rest_n - j, rest_n), qspan(i), :]
            rcopy(there, there, s_re.at[i, j - 1], r_re.at[i, j - 1], rest_peer(j)).wait_recv()
        acc_r = RE[m, 0, qspan(i), :].astype(F32)
        for j in range(1, rest_n):
            acc_r = acc_r + RE[m, j, qspan(i), :].astype(F32)
        here = rxchunk(i, q_id)
        here[...] = acc_r.astype(BF)
        for j in range(1, quad):
            ag_send(i, j).start()

    def reduce_done(i):
        for j in range(1, quad):
            there = rxchunk(i, quad_at(-j))
            rcopy(there, there, s_ag.at[i, j - 1], r_ag.at[i, j - 1], quad_peer(j)).wait_recv()


    def ffn_back(k, carry):
        t = flip(tp, 3 - k)
        d_act = nt(G2L[...], WD[t])
        g_pre = d_act * GP[t].astype(F32)
        SM[pl.ds(10 + t, 1), :] = jnp.sum(g_pre, axis=0, keepdims=True)
        low = g_pre.astype(BF)
        GP[t] = low
        G[0, t] = tn(ACT2[t], G2L[...]).astype(BF)
        G[1, t] = tn(HL[...], low).astype(BF)
        ACC[...] += nt(low, WU[t])

        @pl.when(k == 0)
        def _():
            core_send(0, 1).start()
            core_send(1, 1).start()

        @pl.when(k == 1)
        def _():
            reduce_x(0)
            core_add(1, 1)
            quad_start(1, True)

        @pl.when(k == 2)
        def _():
            core_send(0, 0).start()
            core_send(1, 0).start()

        @pl.when(k == 3)
        def _():
            core_add(1, 0)
            quad_start(1)

        return carry

    lax.fori_loop(0, 4, ffn_back, 0)

    def norm_one_back(i, carry):
        rr = aligned(i, step)
        gh = ACC[rr, :]
        nrm = N1[rr, :]
        gn = gh * gain0
        g1 = LIVE[rr, 1:2] * (
            gn - jnp.mean(gn, axis=-1, keepdims=True) - nrm * jnp.mean(gn * nrm, axis=-1, keepdims=True)
        )
        ACC[rr, :] = g1
        G2L[rr, :] = g1.astype(BF)
        SM[4:5, :] += jnp.sum(gh * nrm, axis=0, keepdims=True)
        SM[6:7, :] += jnp.sum(gh, axis=0, keepdims=True)
        SM[8:9, :] += jnp.sum(g1, axis=0, keepdims=True)
        return carry

    lax.fori_loop(0, 8, norm_one_back, 0)

    def back_prep(p, carry):
        gm = nt(G2L[...], WO[aligned(p, LANES), :])
        WU[p, pl.ds(3 * LANES, LANES), :] = tn(MIX[p], G2L[...]).astype(BF)
        lane_f = lax.broadcasted_iota(jnp.int32, (total, LANES), 1)
        up_f = lane_f >= HD
        gs = gm * LINV[p]
        prod = gs * MIX[p].astype(F32)
        low = gs.astype(BF)
        for e in range(2):
            mine = up_f if e == 1 else jnp.logical_not(up_f)
            delta = jnp.sum(jnp.where(mine, prod, 0.0), axis=-1, keepdims=True)
            hi = delta.astype(BF)
            lo = (delta - hi.astype(F32)).astype(BF)
            base = HD * (1 - e)
            side = jnp.where(lane_f == base, hi, jnp.where(lane_f == base + 1, lo, zero))
            GP[p, :, pl.ds(e * LANES, LANES)] = jnp.where(mine, low, side)
        return carry

    wf_send(2).wait_send()
    for j in range(1, quad):
        wq_send(2, j).wait_send()
    lax.fori_loop(0, 4, back_prep, 0)
    core_send(2, 1).start()
    core_send(2, 0).start()
    reduce_other(1)

    ones = jnp.ones((8, total), BF)
    lane_f = lax.broadcasted_iota(jnp.int32, (total, LANES), 1)
    up_f = lane_f >= HD

    def attend_back(k, carry):
        p = flip(tp, 3 - k)

        def at(where, what):
            @pl.when(k == where)
            def _():
                for fun in what:
                    fun()

        def join(cols, group):
            low = jnp.where(up_f, cols[1], cols[0]).astype(BF)
            ACT2[p, :, group * LANES : (group + 1) * LANES] = low
            WU[p, group * LANES : (group + 1) * LANES, :] = tn(low, ACT[...]).astype(BF)
            SD[p, 0:1, group * LANES : (group + 1) * LANES] = jnp.sum(low.astype(F32), axis=0, keepdims=True)

        def join_t(parts, group):
            low_t = jnp.concatenate([parts[0][:HD], parts[1][HD:]], axis=0).astype(BF)
            WU[p, group * LANES : (group + 1) * LANES, :] = nn(low_t, ACT[...]).astype(BF)
            low = jnp.transpose(low_t)
            ACT2[p, :, group * LANES : (group + 1) * LANES] = low
            SD[p, 0:1, group * LANES : (group + 1) * LANES] = jnp.sum(low.astype(F32), axis=0, keepdims=True)

        def hooks(step):
            for where, todo in enumerate(plan[step]):
                if todo:
                    at(where, todo)

        cols = []
        for e in range(2):
            cols.append(tn(GP[p, :, pl.ds(e * LANES, LANES)], PR[2 * p + e]))
        join_t(cols, 2)
        hooks(0)
        cols = []
        for e in range(2):
            h = 2 * p + e
            for c in range(2):
                rr = pl.ds(c * half, half)
                d_p = nt(GP[p, rr, pl.ds(e * LANES, LANES)], VA[h])
                PR[h, rr, :] = (PR[h, rr, :].astype(F32) * d_p).astype(BF)
            cols.append(tn(QA[h], PR[h]))
        join_t(cols, 1)
        hooks(1)
        cols = []
        for e in range(2):
            h = 2 * p + e
            cols.append(nn(PR[h], KA[h]) * 0.125)
        join(cols, 0)
        hooks(2)
        return carry

    def act(fun, *args):
        return lambda: fun(*args)

    def send(fun, *args):
        return lambda: fun(*args).start()

    plan = (
        (
            (send(core_send, 3, 1), act(reduce_x, 2)),
            (act(reduce_x, 3),),
            (send(core_send, 3, 0), act(reduce_quad, 2)),
            (act(reduce_quad, 3), act(reduce_rest, 2)),
        ),
        (
            (send(core_send, 4, 1),),
            (act(reduce_x, 4),),
            (send(core_send, 4, 0),),
            (act(reduce_quad, 4),),
        ),
        (
            (send(core_send, 5, 1), act(reduce_quad, 0)),
            (act(reduce_x, 5), outs_sent[1].start, act(reduce_rest, 1)),
            (send(core_send, 5, 0), act(reduce_rest, 0)),
            (act(reduce_quad, 5),),
        ),
    )
    lax.fori_loop(0, 4, attend_back, 0)

    base_sum = SM[8:9, :]
    for p in range(4):
        sums = jnp.broadcast_to(SD[p, 0:1, :], (8, 3 * LANES))
        SM[14:15, p * LANES : (p + 1) * LANES] = sums[0:1, 0:LANES]
        SM[15:16, p * LANES : (p + 1) * LANES] = sums[0:1, 2 * LANES : 3 * LANES]
        hi = sums.astype(BF)
        rem = sums - hi.astype(F32)
        mid = rem.astype(BF)
        low = (rem - mid.astype(F32)).astype(BF)
        for term in (hi, mid, low):
            base_sum = base_sum + nt(term, WP[p])[0:1, :]
    for c in range(dbias.shape[0]):
        SM[c : c + 1, :] = jnp.where(ds_here == c, 1.0, 0.0) * base_sum

    stages = (
        (SMT, tp, 4, 0, tp_peer, lambda j: flip(tp, j)),
        (SMQ, q_id, quad, 4, quad_peer, lambda j: quad_at(-j)),
        (SMR, r_id, rest_n, 4 + quad, rest_peer, lambda j: lax.rem(r_id + rest_n - j, rest_n)),
    )

    def sm_send(stage, j):
        slots, me, count, sem0, peer_of, from_of = stages[stage]
        return rcopy(slots.at[me], slots.at[me], s_sm.at[sem0 + j], r_sm.at[sem0 + j], peer_of(j))

    def sm_start(stage, value):
        slots, me, count, sem0, peer_of, from_of = stages[stage]
        slots[me] = value
        for j in range(1, count):
            sm_send(stage, j).start()

    def sm_sum(stage):
        slots, me, count, sem0, peer_of, from_of = stages[stage]
        for j in range(1, count):
            there = slots.at[from_of(j)]
            rcopy(there, there, s_sm.at[sem0 + j], r_sm.at[sem0 + j], peer_of(j)).wait_recv()
        value = slots[0]
        for j in range(1, count):
            value = value + slots[j]
        return value

    sm_start(0, SM[...])
    reduce_gather(1)
    reduce_gather(2)

    def input_grad(k, carry):
        b = flip(tp, 3 - k)
        rr = aligned(b, rows)
        grad = ACC[rr, :]
        for p in range(4):
            grad = grad + nt(ACT2[p, rr, 0 : 3 * LANES], WP[p])
        X[rr, :] = grad.astype(BF)

        @pl.when(k < 3)
        def _():
            kk = 3 - k
            rcopy(X.at[rr, :], ig_rows.at[tp], s_ig.at[kk], r_ig.at[kk], (dp, b)).start()

        return carry

    lax.fori_loop(0, 4, input_grad, 0)
    ig_local = pltpu.make_async_copy(X.at[aligned(tp, rows), :], ig_rows.at[tp], s_loc.at[1])
    ig_local.start()

    sm_start(1, sm_sum(0))
    reduce_rest(3)
    reduce_rest(4)
    reduce_rest(5)
    reduce_gather(0)
    sm_start(2, sm_sum(1))
    reduce_gather(3)
    reduce_gather(4)
    reduce_gather(5)
    g_small[...] = sm_sum(2)
    for i in range(6):
        reduce_done(i)
    result = pltpu.make_async_copy(RX, g_sum, s_res)
    result.start()

    for k in (1, 2, 3):
        back_wait(COT, out_rows, s_out, r_out, k)
        back_wait(X, ig_rows, s_ig, r_ig, k)
        back_copy(X, ig_rows, s_ig, r_ig, k).wait_send()
    ig_local.wait()
    out_local.wait()
    result.wait()
    for copy in sends + outs_sent:
        copy.wait_send()
    for stage in range(3):
        for j in range(1, stages[stage][2]):
            sm_send(stage, j).wait_send()
    for g in (0, 1, 3):
        wf_send(g).wait_send()
        for j in range(1, quad):
            wq_send(g, j).wait_send()
    for i in range(6):
        core_send(i, 0).wait_send()
        core_send(i, 1).wait_send()
        x_send(i).wait_send()
        for j in range(1, quad):
            quad_send(i, j).wait_send()
            ag_send(i, j).wait_send()
            if i == 1:
                quad_send(i, j, True).wait_send()
        for j in range(1, rest_n):
            rest_send(i, j).wait_send()


def finish(
    raw_out, raw_ig, g_sum, g_small,
    out_rows, ig_rows, g_qkv, g_out, g_up, g_down, g_dbias, g_gain, g_shift, g_obias, g_upb, g_qvb,
):
    i = pl.program_id(0)
    tp = lax.axis_index("tp")
    out_rows[...] = raw_out[...]
    ig_rows[...] = raw_ig[...]
    g_down[...] = g_sum[0].astype(F32)
    g_up[...] = g_sum[1].astype(F32)

    @pl.when(i < 3)
    def _():
        g_qkv[0] = jnp.transpose(g_sum[2].astype(F32))

    @pl.when(i == 3)
    def _():
        g_out[...] = g_sum[2].astype(F32)

    @pl.when(i == 0)
    def _():
        g_dbias[...] = g_small[0:4, :]
        g_gain[...] = g_small[4:6, :]
        g_shift[...] = g_small[6:8, :]
        g_obias[...] = g_small[8:10, :]
        g_upb[...] = g_small[pl.ds(10 + tp, 1), :]
        g_qvb[...] = g_small[14:16, aligned(tp, LANES)]


def shards(dp_n, *args):
    (inputs, dataset, variate_mask, dataset_bias, w_qkv, qv_bias, w_out, out_bias, w_up, up_bias, w_down,
     norm_gain, norm_shift, cotangent) = args
    win, rows, width = inputs.shape
    total = variate_mask.shape[1]
    quad = 4 if dp_n <= 16 else 8
    rest_n = dp_n // quad
    ffs = w_up.shape[1]
    assert win == 4 and total == 4 * rows and width == 512 and ffs == 512 and w_out.shape[0] == LANES
    any_spec = pl.BlockSpec(memory_space=pl.ANY)
    vmem = pl.BlockSpec(memory_space=pltpu.VMEM)
    smem = pl.BlockSpec(memory_space=pltpu.SMEM)
    dma = pltpu.SemaphoreType.DMA
    V = pltpu.VMEM
    scratch = [
        V((total, width), BF),
        V((total, width), BF),
        V((4, width, 3 * LANES), BF),
        V((width, width), BF),
        V((4, width, ffs), BF),
        V((4, ffs, width), BF),
        V((4, 8, LANES), F32),
        V((total, width), BF),
        V((8, total, LANES), BF),
        V((8, total, LANES), BF),
        V((8, total, LANES), BF),
        V((8, total, total), BF),
        V((4, total, LANES), BF),
        V((4, total, LANES), F32),
        V((total, width), F32),
        V((total, width), BF),
        V((4, total, ffs), BF),
        V((4, total, ffs), BF),
        V((total, width), F32),
        V((total, width), BF),
        V((total, LANES), F32),
        V((2, 4, width, ffs), BF),
        V((3, 2, width, ffs), BF),
        V((3, width, ffs), BF),
        V((3, quad - 1, width // quad, ffs), BF),
        V((quad - 1, width // quad, ffs), BF),
        V((3, rest_n, width // quad, ffs), BF),
        V((4, 8, 3 * LANES), F32),
        V((16, width), F32),
        V((4, 16, width), F32),
        V((quad, 16, width), F32),
        V((rest_n, 16, width), F32),
        dma((8,)),
        dma((4,)), dma((4,)),
        dma((4,)), dma((4,)),
        dma((6,)), dma((6,)),
        dma((4, quad - 1)), dma((4, quad - 1)),
        dma((4,)), dma((4,)),
        dma((6,)), dma((6,)),
        dma((4,)), dma((4,)),
        dma((4,)), dma((4,)),
        dma((4,)), dma((4,)),
        dma((2,)),
        dma((6, 2)), dma((6, 2)),
        dma((6,)), dma((6,)),
        dma((6, quad - 1)), dma((6, quad - 1)),
        dma((quad - 1,)), dma((quad - 1,)),
        dma((6, max(rest_n - 1, 1))), dma((6, max(rest_n - 1, 1))),
        dma((6, quad - 1)), dma((6, quad - 1)),
        dma((4 + quad + rest_n,)), dma((4 + quad + rest_n,)),
        dma,
    ]
    sds = jax.ShapeDtypeStruct
    outs = pl.pallas_call(
        functools.partial(kernel, quad, rest_n),
        out_shape=(
            sds((win, rows, width), BF),
            sds((win, rows, width), BF),
            sds((3, width, ffs), BF),
            sds((16, width), F32),
        ),
        in_specs=[any_spec, any_spec, smem, vmem, vmem, any_spec, vmem, any_spec, vmem, any_spec, vmem, any_spec, vmem, vmem],
        out_specs=(any_spec,) * 3 + (vmem,),
        scratch_shapes=scratch,
        compiler_params=pltpu.CompilerParams(
            collective_id=0, has_side_effects=True, vmem_limit_bytes=65000000
        ),
        cost_estimate=pl.CostEstimate(flops=30 * 10**9, bytes_accessed=20 * 10**6, transcendentals=10**7),
        name="encoder_layer",
    )(inputs, cotangent, dataset, variate_mask, dataset_bias, w_qkv, qv_bias, w_out, out_bias, w_up,
      up_bias.reshape(4, LANES), w_down, norm_gain, norm_shift)
    raw_out, raw_ig, g_sum, g_small = outs
    res = pl.pallas_call(
        finish,
        out_shape=(
            sds((win, rows, width), BF),
            sds((win, rows, width), BF),
            sds((3, width, LANES), F32),
            sds((LANES, width), F32),
            sds((width, ffs), F32),
            sds((ffs, width), F32),
            sds((4, width), F32),
            sds((2, width), F32),
            sds((2, width), F32),
            sds((2, width), F32),
            sds((1, width), F32),
            sds((2, LANES), F32),
        ),
        grid=(4,),
        in_specs=[
            pl.BlockSpec((1, rows, width), lambda i: (i, 0, 0)),
            pl.BlockSpec((1, rows, width), lambda i: (i, 0, 0)),
            pl.BlockSpec((3, LANES, ffs), lambda i: (0, i, 0)),
            pl.BlockSpec((16, width), lambda i: (0, 0)),
        ],
        out_specs=(
            pl.BlockSpec((1, rows, width), lambda i: (i, 0, 0)),
            pl.BlockSpec((1, rows, width), lambda i: (i, 0, 0)),
            pl.BlockSpec((1, width, LANES), lambda i: (jnp.minimum(i, 2), 0, 0)),
            pl.BlockSpec((LANES, width), lambda i: (0, 0)),
            pl.BlockSpec((LANES, ffs), lambda i: (i, 0)),
            pl.BlockSpec((LANES, width), lambda i: (i, 0)),
            pl.BlockSpec((4, width), lambda i: (0, 0)),
            pl.BlockSpec((2, width), lambda i: (0, 0)),
            pl.BlockSpec((2, width), lambda i: (0, 0)),
            pl.BlockSpec((2, width), lambda i: (0, 0)),
            pl.BlockSpec((1, width), lambda i: (0, 0)),
            pl.BlockSpec((2, LANES), lambda i: (0, 0)),
        ),
        name="write_results",
    )(raw_out, raw_ig, g_sum, g_small)
    (rows_out, rows_ig, g_qkv, g_out, g_up, g_down, g_dbias, g_gain, g_shift, g_obias, g_upb, g_qvb) = res
    return (
        rows_out, rows_ig, g_dbias, g_qkv, g_qvb, g_out, g_obias, g_up, g_upb.reshape(-1), g_down, g_gain, g_shift,
    )


def solution(mesh):
    in_specs = (
        P("dp", "tp", None), P("dp"), P("dp", None), P(), P(None, None, "tp"), P(None, "tp"), P("tp", None), P(),
        P(None, "tp"), P("tp"), P("tp", None), P(), P(), P("dp", "tp", None),
    )
    out_specs = (
        P("dp", "tp", None), P("dp", "tp", None), P(), P(None, None, "tp"), P(None, "tp"), P("tp", None), P(),
        P(None, "tp"), P("tp"), P("tp", None), P(), P(),
    )
    body = functools.partial(shards, mesh.shape["dp"])
    return jax.shard_map(body, mesh=mesh, in_specs=in_specs, out_specs=out_specs, check_vma=False)
```

```python
import functools
import math

import jax
import jax.numpy as jnp
from jax import lax
from jax.experimental import pallas as pl
from jax.experimental.pallas import tpu as pltpu
from jax.sharding import PartitionSpec as P

HD = 64
EPSILON = 1e-05
NEG_FILL = -1e30
BF = jnp.bfloat16
F32 = jnp.float32
MESH = pl.DeviceIdType.MESH
GELU_C = math.sqrt(2.0 / math.pi)
LANES = 128


def nn(a, b):
    return jnp.dot(a, b, preferred_element_type=F32)


def nt(a, b):
    return lax.dot_general(a, b, (((1,), (1,)), ((), ())), preferred_element_type=F32)


def tn(a, b):
    return lax.dot_general(a, b, (((0,), (0,)), ((), ())), preferred_element_type=F32)


def flip(value, k):
    low = lax.rem(lax.rem(value, 2) + k % 2, 2) if isinstance(k, int) else lax.rem(lax.rem(value, 2) + lax.rem(k, 2), 2)
    high = lax.rem(lax.div(value, 2) + (k // 2 if isinstance(k, int) else lax.div(k, 2)), 2)
    return high * 2 + low


def aligned(index, size):
    return pl.ds(pl.multiple_of(index * size, size), size)


def kernel(
    quad, rest_n,
    x_in, cot_in, dataset, mask, dbias, w_qkv, qvb, w_out, obias, w_up, upb, w_down, gain, shift,
    out_rows, ig_rows, g_sum, g_small,
    X, COT, WP, WO, WU, WD, SB, ACT, QA, KA, VA, PR, MIX, LINV, N1, HL, ACT2, GP, ACC, G2L, LIVE,
    G, RC, RX, RQ, RB, RE, SD, SM, SMT, SMQ, SMR,
    s_own, s_x, r_x, s_c, r_c, s_wx, r_wx, s_wq, r_wq, s_wf, r_wf, s_wc, r_wc, s_b, r_b, s_out, r_out, s_ig, r_ig, s_loc,
    s_rc, r_rc, s_rx, r_rx, s_rq, r_rq, s_rb, r_rb, s_re, r_re, s_ag, r_ag, s_sm, r_sm, s_res,
):
    dp = lax.axis_index("dp")
    tp = lax.axis_index("tp")
    q_id = lax.rem(dp, quad)
    r_id = lax.div(dp, quad)
    rows = x_in.shape[1]
    total, width = X.shape
    half = total // 2
    x_id = lax.div(tp, 2)

    def tp_peer(k):
        return (dp, flip(tp, k))

    def quad_at(j):
        return lax.rem(q_id + j + quad, quad)

    def quad_peer(j):
        return (r_id * quad + quad_at(j), tp)

    def rest_peer(j):
        return (lax.rem(r_id + j, rest_n) * quad + q_id, tp)

    def rcopy(src, dst, ss, rs, dev):
        return pltpu.make_async_remote_copy(
            src_ref=src, dst_ref=dst, send_sem=ss, recv_sem=rs, device_id=dev, device_id_type=MESH
        )

    barrier = pltpu.get_barrier_semaphore()
    peers = [tp_peer(k) for k in (1, 2, 3)] + [quad_peer(j) for j in range(1, quad)]
    peers += [rest_peer(j) for j in range(1, rest_n)]
    for peer in peers:
        pl.semaphore_signal(barrier, inc=1, device_id=peer, device_id_type=MESH)

    own = [pltpu.make_async_copy(x_in.at[tp], X.at[aligned(tp, rows), :], s_own.at[0])]
    for i in range(3):
        own.append(pltpu.make_async_copy(w_qkv.at[i], WP.at[tp, :, pl.ds(i * LANES, LANES)], s_own.at[1 + i]))
    own.append(pltpu.make_async_copy(w_out, WO.at[aligned(tp, LANES), :], s_own.at[4]))
    own.append(pltpu.make_async_copy(w_up, WU.at[tp], s_own.at[5]))
    own.append(pltpu.make_async_copy(w_down, WD.at[tp], s_own.at[6]))
    own.append(pltpu.make_async_copy(cot_in.at[tp], COT.at[aligned(tp, rows), :], s_own.at[7]))
    for copy in own:
        copy.start()

    SB[tp, 0:2, :] = qvb[...].astype(F32)
    SB[tp, 2:6, :] = upb[...].astype(F32)
    pl.semaphore_wait(barrier, len(peers))

    wq = width // quad
    oq = LANES // quad

    def w_whole(g, t):
        return (WP.at[t], WO.at[aligned(t, LANES), :], WU.at[t], WD.at[t])[g]

    def w_part(g, t, q):
        if g == 1:
            return WO.at[pl.ds(pl.multiple_of(t * LANES + q * oq, oq), oq), :]
        return (WP, WO, WU, WD)[g].at[t, aligned(q, wq), :]

    def wx_dst(i, t):
        if i < 3:
            return WP.at[t, aligned(q_id, wq), pl.ds(i * LANES, LANES)]
        return w_part(i - 2, t, q_id)

    wx_src = [w_qkv.at[i, aligned(q_id, wq), :] for i in range(3)]
    wx_src += [w_out.at[aligned(q_id, oq), :], w_up.at[aligned(q_id, wq), :], w_down.at[aligned(q_id, wq), :]]
    members = {0: (0, 1, 2), 1: (3,), 2: (4,), 3: (5,)}

    def wx_send(i):
        return rcopy(wx_src[i], wx_dst(i, tp), s_wx.at[i], r_wx.at[i], tp_peer(2))

    def wx_wait(g):
        for i in members[g]:
            there = wx_dst(i, flip(tp, 2))
            rcopy(there, there, s_wx.at[i], r_wx.at[i], tp_peer(2)).wait_recv()

    def wq_send(g, j):
        here = w_part(g, flip(tp, 2), q_id)
        return rcopy(here, here, s_wq.at[g, j - 1], r_wq.at[g, j - 1], quad_peer(j))

    def wq_start(g):
        wx_wait(g)
        for j in range(1, quad):
            wq_send(g, j).start()

    def wf_send(g):
        here = w_whole(g, flip(tp, 2))
        return rcopy(here, here, s_wf.at[g], r_wf.at[g], tp_peer(1))

    def wf_start(g):
        for j in range(1, quad):
            there = w_part(g, flip(tp, 2), quad_at(-j))
            rcopy(there, there, s_wq.at[g, j - 1], r_wq.at[g, j - 1], quad_peer(j)).wait_recv()
        wf_send(g).start()

    def wf_wait(g):
        there = w_whole(g, flip(tp, 3))
        rcopy(there, there, s_wf.at[g], r_wf.at[g], tp_peer(1)).wait_recv()

    def wc_dst(i, t):
        return WP.at[t, :, pl.ds(i * LANES, LANES)] if i < 3 else w_whole(i - 2, t)

    wc_src = [w_qkv.at[0], w_qkv.at[1], w_qkv.at[2], w_out, w_up, w_down]

    def wc_send(i):
        return rcopy(wc_src[i], wc_dst(i, tp), s_wc.at[i], r_wc.at[i], tp_peer(1))

    def wc_wait(g):
        for i in members[g]:
            there = wc_dst(i, flip(tp, 1))
            rcopy(there, there, s_wc.at[i], r_wc.at[i], tp_peer(1)).wait_recv()

    def rows_copy(src, dst, ss, rs, k):
        return rcopy(src.at[flip(tp, k)], dst.at[aligned(tp, rows), :], ss.at[k], rs.at[k], tp_peer(k))

    def rows_wait(dst, ss, rs, k):
        there = dst.at[aligned(flip(tp, k), rows), :]
        rcopy(there, there, ss.at[k], rs.at[k], tp_peer(k)).wait_recv()

    def sb_copy(k):
        return rcopy(SB.at[tp], SB.at[tp], s_b.at[k], r_b.at[k], tp_peer(k))

    sends = []
    for k in (1, 2, 3):
        sends.append(sb_copy(k))
    for i in range(4):
        sends.append(wx_send(i))
    for i in range(4):
        sends.append(wc_send(i))
    for k in (2, 3, 1):
        sends.append(rows_copy(x_in, X, s_x, r_x, k))
    for i in (4, 5):
        sends.append(wx_send(i))
        sends.append(wc_send(i))
    for k in (2, 3, 1):
        sends.append(rows_copy(cot_in, COT, s_c, r_c, k))
    for copy in sends:
        copy.start()

    live_row = mask[pl.ds(tp, 1), :].astype(F32)
    LIVE[:, 0:8] = jnp.transpose(jnp.broadcast_to(live_row, (8, total)))
    ds_here = dataset[tp]
    off = jnp.zeros((1, X.shape[1]), F32)
    for c in range(dbias.shape[0]):
        off = off + jnp.where(ds_here == c, 1.0, 0.0) * dbias[c : c + 1, :].astype(F32)

    for copy in own:
        copy.wait()
    for k in (1, 2, 3):
        there = SB.at[flip(tp, k)]
        rcopy(there, there, s_b.at[k], r_b.at[k], tp_peer(k)).wait_recv()

    lane = lax.broadcasted_iota(jnp.int32, (half, LANES), 1)
    upper = lane >= HD
    one = jnp.ones((), BF)
    zero = jnp.zeros((), BF)

    def project(hh, first):
        rr = aligned(hh, half)
        ACT[rr, :] = (X[rr, :].astype(F32) + off).astype(BF)
        fill = jnp.where(LIVE[rr, 0:1] > 0.5, 0.0, NEG_FILL).astype(BF)
        fill = jnp.broadcast_to(fill, (half, LANES))

        def shard(k, carry):
            t = flip(tp, k)
            if first:
                @pl.when(k == 1)
                def _():
                    wc_wait(0)

                @pl.when(k == 2)
                def _():
                    wf_start(0)
                    wf_start(1)

                @pl.when(k == 3)
                def _():
                    wf_wait(0)

            qkv = nn(ACT[rr, :], WP[t])
            query = (qkv[:, :LANES] + SB[t, 0:1, :]).astype(BF) * BF(0.125)
            keys = qkv[:, LANES : 2 * LANES].astype(BF)
            vals = (qkv[:, 2 * LANES :] + SB[t, 1:2, :]).astype(BF)
            QA[2 * t, rr, :] = jnp.where(upper, jnp.where(lane == HD, one, zero), query)
            QA[2 * t + 1, rr, :] = jnp.where(upper, query, jnp.where(lane == 0, one, zero))
            KA[2 * t, rr, :] = jnp.where(upper, jnp.where(lane == HD, fill, zero), keys)
            KA[2 * t + 1, rr, :] = jnp.where(upper, keys, jnp.where(lane == 0, fill, zero))
            VA[2 * t, rr, :] = jnp.where(upper, -one, vals)
            VA[2 * t + 1, rr, :] = jnp.where(upper, vals, -one)
            return carry

        lax.fori_loop(0, 4, shard, 0)

    wq_start(0)
    wq_start(1)
    rows_wait(X, s_x, r_x, 1)
    project(x_id, True)
    rows_wait(X, s_x, r_x, 2)
    rows_wait(X, s_x, r_x, 3)
    project(1 - x_id, False)

    def attend(p, carry):
        @pl.when(p == 2)
        def _():
            wq_start(2)
            wq_start(3)

        for c in range(2):
            rr = pl.ds(c * half, half)
            outs = []
            for e in range(2):
                h = 2 * p + e
                scores = nt(QA[h, rr, :], KA[h])
                top = jnp.max(scores, axis=1, keepdims=True)
                weight = jnp.exp(scores - top).astype(BF)
                PR[h, rr, :] = weight
                outs.append(nn(weight, VA[h]))
            inv = -1.0 / jnp.where(upper, pltpu.roll(outs[1], HD, 1), pltpu.roll(outs[0], HD, 1))
            LINV[p, rr, :] = inv
            MIX[p, rr, :] = (jnp.where(upper, outs[1], outs[0]) * inv).astype(BF)
        return carry

    lax.fori_loop(0, 4, attend, 0)

    wc_wait(1)
    wf_wait(1)

    acc = nn(MIX[0], WO[0:LANES, :])
    for p in range(1, 4):
        acc = acc + nn(MIX[p], WO[p * LANES : (p + 1) * LANES, :])
    ACC[...] = acc

    step = total // 2
    gain0, gain1 = gain[0:1, :].astype(F32), gain[1:2, :].astype(F32)
    shift0, shift1 = shift[0:1, :].astype(F32), shift[1:2, :].astype(F32)
    ob0, ob1 = obias[0:1, :].astype(F32), obias[1:2, :].astype(F32)

    def norm_one(i, carry):
        rr = aligned(i, step)
        res = X[rr, :].astype(F32) + off + (ACC[rr, :] + ob0)
        cen = res - jnp.mean(res, axis=-1, keepdims=True)
        fac = lax.rsqrt(jnp.mean(cen * cen, axis=-1, keepdims=True) + EPSILON)
        nrm = cen * fac
        N1[rr, :] = nrm
        LIVE[rr, 1:2] = fac
        HL[rr, :] = (nrm * gain0 + shift0).astype(BF)
        return carry

    lax.fori_loop(0, 2, norm_one, 0)

    ACC[...] = jnp.zeros_like(ACC)

    def ffn(k, carry):
        t = flip(tp, k)

        @pl.when(k == 1)
        def _():
            wc_wait(2)
            wc_wait(3)

        @pl.when(k == 2)
        def _():
            wf_start(2)
            wf_start(3)

        @pl.when(k == 3)
        def _():
            wf_wait(2)
            wf_wait(3)

        for c in range(2):
            rr = pl.ds(c * half, half)
            upper_bias = jnp.concatenate([SB[t, 2 + i : 3 + i, :] for i in range(4)], axis=1)
            u = nn(HL[rr, :], WU[t]) + upper_bias
            sq = u * u
            th = jnp.tanh(u * (GELU_C + (GELU_C * 0.044715) * sq))
            hp = 0.5 + 0.5 * th
            act = (u * hp).astype(BF)
            ACT2[t, rr, :] = act
            GP[t, rr, :] = (
                hp + (0.5 * u) * (1.0 - th * th) * (GELU_C + (3.0 * GELU_C * 0.044715) * sq)
            ).astype(BF)
            ACC[rr, :] += nn(act, WD[t])
        return carry

    lax.fori_loop(0, 4, ffn, 0)

    for k in (1, 2, 3):
        rows_wait(COT, s_c, r_c, k)

    SM[...] = jnp.zeros_like(SM)

    def norm_two(i, carry):
        rr = aligned(i, step)
        hid = N1[rr, :] * gain0 + shift0
        res = hid + (ACC[rr, :] + ob1)
        cen = res - jnp.mean(res, axis=-1, keepdims=True)
        fac = lax.rsqrt(jnp.mean(cen * cen, axis=-1, keepdims=True) + EPSILON)
        nrm = cen * fac
        live = LIVE[rr, 0:1]
        gf = COT[rr, :].astype(F32) * live
        COT[rr, :] = ((nrm * gain1 + shift1) * live).astype(BF)
        gn = gf * gain1
        g2 = fac * (
            gn - jnp.mean(gn, axis=-1, keepdims=True) - nrm * jnp.mean(gn * nrm, axis=-1, keepdims=True)
        )
        ACC[rr, :] = g2
        G2L[rr, :] = g2.astype(BF)
        SM[5:6, :] += jnp.sum(gf * nrm, axis=0, keepdims=True)
        SM[7:8, :] += jnp.sum(gf, axis=0, keepdims=True)
        SM[9:10, :] += jnp.sum(g2, axis=0, keepdims=True)
        return carry

    lax.fori_loop(0, 2, norm_two, 0)

    def back_copy(buf, dst, ss, rs, k):
        return rcopy(buf.at[aligned(flip(tp, k), rows), :], dst.at[tp], ss.at[k], rs.at[k], tp_peer(k))

    def back_wait(buf, dst, ss, rs, k):
        there = dst.at[flip(tp, k)]
        rcopy(buf.at[aligned(tp, rows), :], there, ss.at[k], rs.at[k], tp_peer(k)).wait_recv()

    outs_sent = [back_copy(COT, out_rows, s_out, r_out, k) for k in (2, 3, 1)]
    outs_sent[0].start()
    outs_sent[2].start()
    out_local = pltpu.make_async_copy(COT.at[aligned(tp, rows), :], out_rows.at[tp], s_loc.at[0])
    out_local.start()

    pieces = ((0, 0, width), (1, 0, width)) + tuple((2, g * LANES, LANES) for g in (3, 2, 1, 0))

    def gref(i, t):
        m, r0, n = pieces[i]
        return WU.at[t, pl.ds(r0, n), :] if m == 2 else G.at[m, t]

    def gchunk(i, t, q):
        m, r0, n = pieces[i]
        at = pl.ds(pl.multiple_of(r0 + q * (n // quad), 16), n // quad)
        return WU.at[t, at, :] if m == 2 else G.at[m, t, at, :]

    def rxchunk(i, q):
        m, r0, n = pieces[i]
        return RX.at[m, pl.ds(pl.multiple_of(r0 + q * (n // quad), 16), n // quad), :]

    def span(i):
        return pl.ds(pieces[i][1], pieces[i][2])

    def qspan(i):
        return pl.ds(pieces[i][1] // quad, pieces[i][2] // quad)

    def core_send(i, j):
        there = RC.at[pieces[i][0], j, span(i), :]
        return rcopy(gref(i, flip(tp, 1 if j == 0 else 3)), there, s_rc.at[i, j], r_rc.at[i, j], tp_peer(1))

    def core_add(i, j):
        there = RC.at[pieces[i][0], j, span(i), :]
        rcopy(there, there, s_rc.at[i, j], r_rc.at[i, j], tp_peer(1)).wait_recv()
        ref = gref(i, flip(tp, 2) if j == 1 else tp)
        ref[...] = (ref[...].astype(F32) + there[...].astype(F32)).astype(BF)

    def x_send(i):
        if i == 1:
            src, dst = gchunk(i, flip(tp, 2), q_id), rxchunk(i, q_id)
        else:
            src, dst = gref(i, flip(tp, 2)), RX.at[pieces[i][0], span(i), :]
        return rcopy(src, dst, s_rx.at[i], r_rx.at[i], tp_peer(2))

    def quad_send(i, j, other=False):
        if other:
            return rcopy(gchunk(i, flip(tp, 2), quad_at(j)), RB.at[j - 1], s_rb.at[j - 1], r_rb.at[j - 1], quad_peer(j))
        there = RQ.at[pieces[i][0], j - 1, qspan(i), :]
        return rcopy(gchunk(i, tp, quad_at(j)), there, s_rq.at[i, j - 1], r_rq.at[i, j - 1], quad_peer(j))

    def quad_start(i, other=False):
        for j in range(1, quad):
            quad_send(i, j, other).start()

    def rest_send(i, j):
        here = RE.at[pieces[i][0], r_id, qspan(i), :]
        return rcopy(here, here, s_re.at[i, j - 1], r_re.at[i, j - 1], rest_peer(j))

    def ag_send(i, j):
        here = rxchunk(i, q_id)
        return rcopy(here, here, s_ag.at[i, j - 1], r_ag.at[i, j - 1], quad_peer(j))

    def reduce_x(i):
        core_add(i, 1)
        x_send(i).start()

    def reduce_quad(i):
        core_add(i, 0)
        x_send(i).wait_recv()
        ref = gref(i, tp)
        ref[...] = (ref[...].astype(F32) + RX[pieces[i][0], span(i), :].astype(F32)).astype(BF)
        quad_start(i)

    def reduce_other(i):
        for j in range(1, quad):
            quad_send(i, j, True).wait_recv()
        ref = gchunk(i, flip(tp, 2), q_id)
        acc_q = ref[...].astype(F32)
        for j in range(quad - 1):
            acc_q = acc_q + RB[j].astype(F32)
        ref[...] = acc_q.astype(BF)
        x_send(i).start()

    def reduce_rest(i):
        m = pieces[i][0]
        for j in range(1, quad):
            quad_send(i, j).wait_recv()
        acc_q = gchunk(i, tp, q_id)[...].astype(F32)
        for j in range(quad - 1):
            acc_q = acc_q + RQ[m, j, qspan(i), :].astype(F32)
        if i == 1:
            x_send(i).wait_recv()
            acc_q = acc_q + rxchunk(i, q_id)[...].astype(F32)
        RE[m, r_id, qspan(i), :] = acc_q.astype(BF)
        for j in range(1, rest_n):
            rest_send(i, j).start()

    def reduce_gather(i):
        m = pieces[i][0]
        for j in range(1, rest_n):
            there = RE.at[m, lax.rem(r_id + rest_n - j, rest_n), qspan(i), :]
            rcopy(there, there, s_re.at[i, j - 1], r_re.at[i, j - 1], rest_peer(j)).wait_recv()
        acc_r = RE[m, 0, qspan(i), :].astype(F32)
        for j in range(1, rest_n):
            acc_r = acc_r + RE[m, j, qspan(i), :].astype(F32)
        here = rxchunk(i, q_id)
        here[...] = acc_r.astype(BF)
        for j in range(1, quad):
            ag_send(i, j).start()

    def reduce_done(i):
        for j in range(1, quad):
            there = rxchunk(i, quad_at(-j))
            rcopy(there, there, s_ag.at[i, j - 1], r_ag.at[i, j - 1], quad_peer(j)).wait_recv()


    def ffn_back(k, carry):
        t = flip(tp, 3 - k)
        d_act = nt(G2L[...], WD[t])
        g_pre = d_act * GP[t].astype(F32)
        SM[pl.ds(10 + t, 1), :] = jnp.sum(g_pre, axis=0, keepdims=True)
        low = g_pre.astype(BF)
        GP[t] = low
        G[0, t] = tn(ACT2[t], G2L[...]).astype(BF)
        G[1, t] = tn(HL[...], low).astype(BF)
        ACC[...] += nt(low, WU[t])

        @pl.when(k == 0)
        def _():
            core_send(0, 1).start()
            core_send(1, 1).start()

        @pl.when(k == 1)
        def _():
            reduce_x(0)
            core_add(1, 1)
            quad_start(1, True)

        @pl.when(k == 2)
        def _():
            core_send(0, 0).start()
            core_send(1, 0).start()

        @pl.when(k == 3)
        def _():
            core_add(1, 0)
            quad_start(1)

        return carry

    lax.fori_loop(0, 4, ffn_back, 0)

    def norm_one_back(i, carry):
        rr = aligned(i, step)
        gh = ACC[rr, :]
        nrm = N1[rr, :]
        gn = gh * gain0
        g1 = LIVE[rr, 1:2] * (
            gn - jnp.mean(gn, axis=-1, keepdims=True) - nrm * jnp.mean(gn * nrm, axis=-1, keepdims=True)
        )
        ACC[rr, :] = g1
        G2L[rr, :] = g1.astype(BF)
        SM[4:5, :] += jnp.sum(gh * nrm, axis=0, keepdims=True)
        SM[6:7, :] += jnp.sum(gh, axis=0, keepdims=True)
        SM[8:9, :] += jnp.sum(g1, axis=0, keepdims=True)
        return carry

    lax.fori_loop(0, 2, norm_one_back, 0)

    def back_prep(p, carry):
        gm = nt(G2L[...], WO[aligned(p, LANES), :])
        WU[p, pl.ds(3 * LANES, LANES), :] = tn(MIX[p], G2L[...]).astype(BF)
        lane_f = lax.broadcasted_iota(jnp.int32, (total, LANES), 1)
        up_f = lane_f >= HD
        gs = gm * LINV[p]
        prod = gs * MIX[p].astype(F32)
        low = gs.astype(BF)
        for e in range(2):
            mine = up_f if e == 1 else jnp.logical_not(up_f)
            delta = jnp.sum(jnp.where(mine, prod, 0.0), axis=-1, keepdims=True)
            hi = delta.astype(BF)
            lo = (delta - hi.astype(F32)).astype(BF)
            base = HD * (1 - e)
            side = jnp.where(lane_f == base, hi, jnp.where(lane_f == base + 1, lo, zero))
            GP[p, :, pl.ds(e * LANES, LANES)] = jnp.where(mine, low, side)
        return carry

    wf_send(2).wait_send()
    for j in range(1, quad):
        wq_send(2, j).wait_send()
    lax.fori_loop(0, 4, back_prep, 0)
    core_send(2, 1).start()
    core_send(2, 0).start()
    reduce_other(1)

    ones = jnp.ones((8, total), BF)
    lane_f = lax.broadcasted_iota(jnp.int32, (total, LANES), 1)
    up_f = lane_f >= HD

    def attend_back(k, carry):
        p = flip(tp, 3 - k)

        def at(where, what):
            @pl.when(k == where)
            def _():
                for fun in what:
                    fun()

        def join(cols, group):
            low = jnp.where(up_f, cols[1], cols[0]).astype(BF)
            ACT2[p, :, group * LANES : (group + 1) * LANES] = low
            WU[p, group * LANES : (group + 1) * LANES, :] = tn(low, ACT[...]).astype(BF)
            SD[p, 0:1, group * LANES : (group + 1) * LANES] = jnp.sum(low.astype(F32), axis=0, keepdims=True)

        def join_t(parts, group):
            low_t = jnp.concatenate([parts[0][:HD], parts[1][HD:]], axis=0).astype(BF)
            WU[p, group * LANES : (group + 1) * LANES, :] = nn(low_t, ACT[...]).astype(BF)
            low = jnp.transpose(low_t)
            ACT2[p, :, group * LANES : (group + 1) * LANES] = low
            SD[p, 0:1, group * LANES : (group + 1) * LANES] = jnp.sum(low.astype(F32), axis=0, keepdims=True)

        def hooks(step):
            for where, todo in enumerate(plan[step]):
                if todo:
                    at(where, todo)

        cols = []
        for e in range(2):
            cols.append(tn(GP[p, :, pl.ds(e * LANES, LANES)], PR[2 * p + e]))
        join_t(cols, 2)
        hooks(0)
        cols = []
        for e in range(2):
            h = 2 * p + e
            for c in range(2):
                rr = pl.ds(c * half, half)
                d_p = nt(GP[p, rr, pl.ds(e * LANES, LANES)], VA[h])
                PR[h, rr, :] = (PR[h, rr, :].astype(F32) * d_p).astype(BF)
            cols.append(tn(QA[h], PR[h]))
        join_t(cols, 1)
        hooks(1)
        cols = []
        for e in range(2):
            h = 2 * p + e
            cols.append(nn(PR[h], KA[h]) * 0.125)
        join(cols, 0)
        hooks(2)
        return carry

    def act(fun, *args):
        return lambda: fun(*args)

    def send(fun, *args):
        return lambda: fun(*args).start()

    plan = (
        (
            (send(core_send, 3, 1), act(reduce_x, 2)),
            (act(reduce_x, 3),),
            (send(core_send, 3, 0), act(reduce_quad, 2)),
            (act(reduce_quad, 3), act(reduce_rest, 2)),
        ),
        (
            (send(core_send, 4, 1),),
            (act(reduce_x, 4),),
            (send(core_send, 4, 0),),
            (act(reduce_quad, 4),),
        ),
        (
            (send(core_send, 5, 1), act(reduce_quad, 0)),
            (act(reduce_x, 5), outs_sent[1].start, act(reduce_rest, 1)),
            (send(core_send, 5, 0), act(reduce_rest, 0)),
            (act(reduce_quad, 5),),
        ),
    )
    lax.fori_loop(0, 4, attend_back, 0)

    base_sum = SM[8:9, :]
    for p in range(4):
        sums = jnp.broadcast_to(SD[p, 0:1, :], (8, 3 * LANES))
        SM[14:15, p * LANES : (p + 1) * LANES] = sums[0:1, 0:LANES]
        SM[15:16, p * LANES : (p + 1) * LANES] = sums[0:1, 2 * LANES : 3 * LANES]
        hi = sums.astype(BF)
        rem = sums - hi.astype(F32)
        mid = rem.astype(BF)
        low = (rem - mid.astype(F32)).astype(BF)
        for term in (hi, mid, low):
            base_sum = base_sum + nt(term, WP[p])[0:1, :]
    for c in range(dbias.shape[0]):
        SM[c : c + 1, :] = jnp.where(ds_here == c, 1.0, 0.0) * base_sum

    stages = (
        (SMT, tp, 4, 0, tp_peer, lambda j: flip(tp, j)),
        (SMQ, q_id, quad, 4, quad_peer, lambda j: quad_at(-j)),
        (SMR, r_id, rest_n, 4 + quad, rest_peer, lambda j: lax.rem(r_id + rest_n - j, rest_n)),
    )

    def sm_send(stage, j):
        slots, me, count, sem0, peer_of, from_of = stages[stage]
        return rcopy(slots.at[me], slots.at[me], s_sm.at[sem0 + j], r_sm.at[sem0 + j], peer_of(j))

    def sm_start(stage, value):
        slots, me, count, sem0, peer_of, from_of = stages[stage]
        slots[me] = value
        for j in range(1, count):
            sm_send(stage, j).start()

    def sm_sum(stage):
        slots, me, count, sem0, peer_of, from_of = stages[stage]
        for j in range(1, count):
            there = slots.at[from_of(j)]
            rcopy(there, there, s_sm.at[sem0 + j], r_sm.at[sem0 + j], peer_of(j)).wait_recv()
        value = slots[0]
        for j in range(1, count):
            value = value + slots[j]
        return value

    sm_start(0, SM[...])
    reduce_gather(1)
    reduce_gather(2)

    def input_grad(k, carry):
        b = flip(tp, 3 - k)
        rr = aligned(b, rows)
        grad = ACC[rr, :]
        for p in range(4):
            grad = grad + nt(ACT2[p, rr, 0 : 3 * LANES], WP[p])
        X[rr, :] = grad.astype(BF)

        @pl.when(k < 3)
        def _():
            kk = 3 - k
            rcopy(X.at[rr, :], ig_rows.at[tp], s_ig.at[kk], r_ig.at[kk], (dp, b)).start()

        return carry

    lax.fori_loop(0, 4, input_grad, 0)
    ig_local = pltpu.make_async_copy(X.at[aligned(tp, rows), :], ig_rows.at[tp], s_loc.at[1])
    ig_local.start()

    sm_start(1, sm_sum(0))
    reduce_rest(3)
    reduce_rest(4)
    reduce_rest(5)
    reduce_gather(0)
    sm_start(2, sm_sum(1))
    reduce_gather(3)
    reduce_gather(4)
    reduce_gather(5)
    results = []
    for m, done in enumerate(((0,), (1,), (2, 3, 4, 5))):
        for i in done:
            reduce_done(i)
        results.append(pltpu.make_async_copy(RX.at[m], g_sum.at[m], s_res.at[m]))
        results[-1].start()

    g_small[...] = sm_sum(2)
    for k in (1, 2, 3):
        back_wait(COT, out_rows, s_out, r_out, k)
        back_wait(X, ig_rows, s_ig, r_ig, k)
        back_copy(X, ig_rows, s_ig, r_ig, k).wait_send()
    ig_local.wait()
    out_local.wait()
    for result in results:
        result.wait()
    for copy in sends + outs_sent:
        copy.wait_send()
    for stage in range(3):
        for j in range(1, stages[stage][2]):
            sm_send(stage, j).wait_send()
    for g in (0, 1, 3):
        wf_send(g).wait_send()
        for j in range(1, quad):
            wq_send(g, j).wait_send()
    for i in range(6):
        core_send(i, 0).wait_send()
        core_send(i, 1).wait_send()
        x_send(i).wait_send()
        for j in range(1, quad):
            quad_send(i, j).wait_send()
            ag_send(i, j).wait_send()
            if i == 1:
                quad_send(i, j, True).wait_send()
        for j in range(1, rest_n):
            rest_send(i, j).wait_send()


def finish(
    raw_out, raw_ig, g_sum, g_small,
    out_rows, ig_rows, g_qkv, g_out, g_up, g_down, g_dbias, g_gain, g_shift, g_obias, g_upb, g_qvb,
):
    i = pl.program_id(0)
    tp = lax.axis_index("tp")
    out_rows[...] = raw_out[...]
    ig_rows[...] = raw_ig[...]
    g_down[...] = g_sum[0].astype(F32)
    g_up[...] = g_sum[1].astype(F32)

    @pl.when(i < 3)
    def _():
        g_qkv[0] = jnp.transpose(g_sum[2].astype(F32))

    @pl.when(i == 3)
    def _():
        g_out[...] = g_sum[2].astype(F32)

    @pl.when(i == 0)
    def _():
        g_dbias[...] = g_small[0:4, :]
        g_gain[...] = g_small[4:6, :]
        g_shift[...] = g_small[6:8, :]
        g_obias[...] = g_small[8:10, :]
        g_upb[...] = g_small[pl.ds(10 + tp, 1), :]
        g_qvb[...] = g_small[14:16, aligned(tp, LANES)]


def shards(dp_n, *args):
    (inputs, dataset, variate_mask, dataset_bias, w_qkv, qv_bias, w_out, out_bias, w_up, up_bias, w_down,
     norm_gain, norm_shift, cotangent) = args
    win, rows, width = inputs.shape
    total = variate_mask.shape[1]
    quad = 4 if dp_n <= 16 else 8
    rest_n = dp_n // quad
    ffs = w_up.shape[1]
    assert win == 4 and total == 4 * rows and width == 512 and ffs == 512 and w_out.shape[0] == LANES
    any_spec = pl.BlockSpec(memory_space=pl.ANY)
    vmem = pl.BlockSpec(memory_space=pltpu.VMEM)
    smem = pl.BlockSpec(memory_space=pltpu.SMEM)
    dma = pltpu.SemaphoreType.DMA
    V = pltpu.VMEM
    scratch = [
        V((total, width), BF),
        V((total, width), BF),
        V((4, width, 3 * LANES), BF),
        V((width, width), BF),
        V((4, width, ffs), BF),
        V((4, ffs, width), BF),
        V((4, 8, LANES), F32),
        V((total, width), BF),
        V((8, total, LANES), BF),
        V((8, total, LANES), BF),
        V((8, total, LANES), BF),
        V((8, total, total), BF),
        V((4, total, LANES), BF),
        V((4, total, LANES), F32),
        V((total, width), F32),
        V((total, width), BF),
        V((4, total, ffs), BF),
        V((4, total, ffs), BF),
        V((total, width), F32),
        V((total, width), BF),
        V((total, LANES), F32),
        V((2, 4, width, ffs), BF),
        V((3, 2, width, ffs), BF),
        V((3, width, ffs), BF),
        V((3, quad - 1, width // quad, ffs), BF),
        V((quad - 1, width // quad, ffs), BF),
        V((3, rest_n, width // quad, ffs), BF),
        V((4, 8, 3 * LANES), F32),
        V((16, width), F32),
        V((4, 16, width), F32),
        V((quad, 16, width), F32),
        V((rest_n, 16, width), F32),
        dma((8,)),
        dma((4,)), dma((4,)),
        dma((4,)), dma((4,)),
        dma((6,)), dma((6,)),
        dma((4, quad - 1)), dma((4, quad - 1)),
        dma((4,)), dma((4,)),
        dma((6,)), dma((6,)),
        dma((4,)), dma((4,)),
        dma((4,)), dma((4,)),
        dma((4,)), dma((4,)),
        dma((2,)),
        dma((6, 2)), dma((6, 2)),
        dma((6,)), dma((6,)),
        dma((6, quad - 1)), dma((6, quad - 1)),
        dma((quad - 1,)), dma((quad - 1,)),
        dma((6, max(rest_n - 1, 1))), dma((6, max(rest_n - 1, 1))),
        dma((6, quad - 1)), dma((6, quad - 1)),
        dma((4 + quad + rest_n,)), dma((4 + quad + rest_n,)),
        dma((3,)),
    ]
    sds = jax.ShapeDtypeStruct
    outs = pl.pallas_call(
        functools.partial(kernel, quad, rest_n),
        out_shape=(
            sds((win, rows, width), BF),
            sds((win, rows, width), BF),
            sds((3, width, ffs), BF),
            sds((16, width), F32),
        ),
        in_specs=[any_spec, any_spec, smem, vmem, vmem, any_spec, vmem, any_spec, vmem, any_spec, vmem, any_spec, vmem, vmem],
        out_specs=(any_spec,) * 3 + (vmem,),
        scratch_shapes=scratch,
        compiler_params=pltpu.CompilerParams(
            collective_id=0, has_side_effects=True, vmem_limit_bytes=65000000
        ),
        cost_estimate=pl.CostEstimate(flops=30 * 10**9, bytes_accessed=20 * 10**6, transcendentals=10**7),
        name="encoder_layer",
    )(inputs, cotangent, dataset, variate_mask, dataset_bias, w_qkv, qv_bias, w_out, out_bias, w_up,
      up_bias.reshape(4, LANES), w_down, norm_gain, norm_shift)
    raw_out, raw_ig, g_sum, g_small = outs
    res = pl.pallas_call(
        finish,
        out_shape=(
            sds((win, rows, width), BF),
            sds((win, rows, width), BF),
            sds((3, width, LANES), F32),
            sds((LANES, width), F32),
            sds((width, ffs), F32),
            sds((ffs, width), F32),
            sds((4, width), F32),
            sds((2, width), F32),
            sds((2, width), F32),
            sds((2, width), F32),
            sds((1, width), F32),
            sds((2, LANES), F32),
        ),
        grid=(4,),
        in_specs=[
            pl.BlockSpec((1, rows, width), lambda i: (i, 0, 0)),
            pl.BlockSpec((1, rows, width), lambda i: (i, 0, 0)),
            pl.BlockSpec((3, LANES, ffs), lambda i: (0, i, 0)),
            pl.BlockSpec((16, width), lambda i: (0, 0)),
        ],
        out_specs=(
            pl.BlockSpec((1, rows, width), lambda i: (i, 0, 0)),
            pl.BlockSpec((1, rows, width), lambda i: (i, 0, 0)),
            pl.BlockSpec((1, width, LANES), lambda i: (jnp.minimum(i, 2), 0, 0)),
            pl.BlockSpec((LANES, width), lambda i: (0, 0)),
            pl.BlockSpec((LANES, ffs), lambda i: (i, 0)),
            pl.BlockSpec((LANES, width), lambda i: (i, 0)),
            pl.BlockSpec((4, width), lambda i: (0, 0)),
            pl.BlockSpec((2, width), lambda i: (0, 0)),
            pl.BlockSpec((2, width), lambda i: (0, 0)),
            pl.BlockSpec((2, width), lambda i: (0, 0)),
            pl.BlockSpec((1, width), lambda i: (0, 0)),
            pl.BlockSpec((2, LANES), lambda i: (0, 0)),
        ),
        name="write_results",
    )(raw_out, raw_ig, g_sum, g_small)
    (rows_out, rows_ig, g_qkv, g_out, g_up, g_down, g_dbias, g_gain, g_shift, g_obias, g_upb, g_qvb) = res
    return (
        rows_out, rows_ig, g_dbias, g_qkv, g_qvb, g_out, g_obias, g_up, g_upb.reshape(-1), g_down, g_gain, g_shift,
    )


def solution(mesh):
    in_specs = (
        P("dp", "tp", None), P("dp"), P("dp", None), P(), P(None, None, "tp"), P(None, "tp"), P("tp", None), P(),
        P(None, "tp"), P("tp"), P("tp", None), P(), P(), P("dp", "tp", None),
    )
    out_specs = (
        P("dp", "tp", None), P("dp", "tp", None), P(), P(None, None, "tp"), P(None, "tp"), P("tp", None), P(),
        P(None, "tp"), P("tp"), P("tp", None), P(), P(),
    )
    body = functools.partial(shards, mesh.shape["dp"])
    return jax.shard_map(body, mesh=mesh, in_specs=in_specs, out_specs=out_specs, check_vma=False)
```

```python
import functools
import math

import jax
import jax.numpy as jnp
from jax import lax
from jax.experimental import pallas as pl
from jax.experimental.pallas import tpu as pltpu
from jax.sharding import PartitionSpec as P

HD = 64
EPSILON = 1e-05
NEG_FILL = -1e30
BF = jnp.bfloat16
F32 = jnp.float32
MESH = pl.DeviceIdType.MESH
GELU_C = math.sqrt(2.0 / math.pi)
LANES = 128


def nn(a, b):
    return jnp.dot(a, b, preferred_element_type=F32)


def nt(a, b):
    return lax.dot_general(a, b, (((1,), (1,)), ((), ())), preferred_element_type=F32)


def tn(a, b):
    return lax.dot_general(a, b, (((0,), (0,)), ((), ())), preferred_element_type=F32)


def flip(value, k):
    low = lax.rem(lax.rem(value, 2) + k % 2, 2) if isinstance(k, int) else lax.rem(lax.rem(value, 2) + lax.rem(k, 2), 2)
    high = lax.rem(lax.div(value, 2) + (k // 2 if isinstance(k, int) else lax.div(k, 2)), 2)
    return high * 2 + low


def aligned(index, size):
    return pl.ds(pl.multiple_of(index * size, size), size)


def kernel(
    quad, rest_n,
    x_in, cot_in, dataset, mask, dbias, w_qkv, qvb, w_out, obias, w_up, upb, w_down, gain, shift,
    out_rows, ig_rows, g_sum, g_small,
    X, COT, WP, WO, WU, WD, SB, ACT, QA, KA, VA, PR, MIX, LINV, N1, HL, ACT2, GP, ACC, G2L, LIVE,
    G, RC, RX, RQ, RB, RE, SD, SM, SMT, SMQ, SMR,
    s_own, s_x, r_x, s_c, r_c, s_wx, r_wx, s_wq, r_wq, s_wf, r_wf, s_wc, r_wc, s_b, r_b, s_out, r_out, s_ig, r_ig, s_loc,
    s_rc, r_rc, s_rx, r_rx, s_rq, r_rq, s_rb, r_rb, s_re, r_re, s_ag, r_ag, s_sm, r_sm, s_res,
):
    dp = lax.axis_index("dp")
    tp = lax.axis_index("tp")
    q_id = lax.rem(dp, quad)
    r_id = lax.div(dp, quad)
    rows = x_in.shape[1]
    total, width = X.shape
    half = total // 2
    x_id = lax.div(tp, 2)

    def tp_peer(k):
        return (dp, flip(tp, k))

    def quad_at(j):
        return lax.rem(q_id + j + quad, quad)

    def quad_peer(j):
        return (r_id * quad + quad_at(j), tp)

    def rest_peer(j):
        return (lax.rem(r_id + j, rest_n) * quad + q_id, tp)

    def rcopy(src, dst, ss, rs, dev):
        return pltpu.make_async_remote_copy(
            src_ref=src, dst_ref=dst, send_sem=ss, recv_sem=rs, device_id=dev, device_id_type=MESH
        )

    barrier = pltpu.get_barrier_semaphore()
    peers = [tp_peer(k) for k in (1, 2, 3)] + [quad_peer(j) for j in range(1, quad)]
    peers += [rest_peer(j) for j in range(1, rest_n)]
    for peer in peers:
        pl.semaphore_signal(barrier, inc=1, device_id=peer, device_id_type=MESH)

    own = [pltpu.make_async_copy(x_in.at[tp], X.at[aligned(tp, rows), :], s_own.at[0])]
    for i in range(3):
        own.append(pltpu.make_async_copy(w_qkv.at[i], WP.at[tp, :, pl.ds(i * LANES, LANES)], s_own.at[1 + i]))
    own.append(pltpu.make_async_copy(w_out, WO.at[aligned(tp, LANES), :], s_own.at[4]))
    own.append(pltpu.make_async_copy(w_up, WU.at[tp], s_own.at[5]))
    own.append(pltpu.make_async_copy(w_down, WD.at[tp], s_own.at[6]))
    own.append(pltpu.make_async_copy(cot_in.at[tp], COT.at[aligned(tp, rows), :], s_own.at[7]))
    for copy in own:
        copy.start()

    SB[tp, 0:2, :] = qvb[...].astype(F32)
    SB[tp, 2:6, :] = upb[...].astype(F32)
    pl.semaphore_wait(barrier, len(peers))

    wq = width // quad
    oq = LANES // quad

    def w_whole(g, t):
        return (WP.at[t], WO.at[aligned(t, LANES), :], WU.at[t], WD.at[t])[g]

    def w_part(g, t, q):
        if g == 1:
            return WO.at[pl.ds(pl.multiple_of(t * LANES + q * oq, oq), oq), :]
        return (WP, WO, WU, WD)[g].at[t, aligned(q, wq), :]

    def wx_dst(i, t):
        if i < 3:
            return WP.at[t, aligned(q_id, wq), pl.ds(i * LANES, LANES)]
        return w_part(i - 2, t, q_id)

    wx_src = [w_qkv.at[i, aligned(q_id, wq), :] for i in range(3)]
    wx_src += [w_out.at[aligned(q_id, oq), :], w_up.at[aligned(q_id, wq), :], w_down.at[aligned(q_id, wq), :]]
    members = {0: (0, 1, 2), 1: (3,), 2: (4,), 3: (5,)}

    def wx_send(i):
        return rcopy(wx_src[i], wx_dst(i, tp), s_wx.at[i], r_wx.at[i], tp_peer(2))

    def wx_wait(g):
        for i in members[g]:
            there = wx_dst(i, flip(tp, 2))
            rcopy(there, there, s_wx.at[i], r_wx.at[i], tp_peer(2)).wait_recv()

    def wq_send(g, j):
        here = w_part(g, flip(tp, 2), q_id)
        return rcopy(here, here, s_wq.at[g, j - 1], r_wq.at[g, j - 1], quad_peer(j))

    def wq_start(g):
        wx_wait(g)
        for j in range(1, quad):
            wq_send(g, j).start()

    def wf_send(g):
        here = w_whole(g, flip(tp, 2))
        return rcopy(here, here, s_wf.at[g], r_wf.at[g], tp_peer(1))

    def wf_start(g):
        for j in range(1, quad):
            there = w_part(g, flip(tp, 2), quad_at(-j))
            rcopy(there, there, s_wq.at[g, j - 1], r_wq.at[g, j - 1], quad_peer(j)).wait_recv()
        wf_send(g).start()

    def wf_wait(g):
        there = w_whole(g, flip(tp, 3))
        rcopy(there, there, s_wf.at[g], r_wf.at[g], tp_peer(1)).wait_recv()

    def wc_dst(i, t):
        return WP.at[t, :, pl.ds(i * LANES, LANES)] if i < 3 else w_whole(i - 2, t)

    wc_src = [w_qkv.at[0], w_qkv.at[1], w_qkv.at[2], w_out, w_up, w_down]

    def wc_send(i):
        return rcopy(wc_src[i], wc_dst(i, tp), s_wc.at[i], r_wc.at[i], tp_peer(1))

    def wc_wait(g):
        for i in members[g]:
            there = wc_dst(i, flip(tp, 1))
            rcopy(there, there, s_wc.at[i], r_wc.at[i], tp_peer(1)).wait_recv()

    def rows_copy(src, dst, ss, rs, k):
        return rcopy(src.at[flip(tp, k)], dst.at[aligned(tp, rows), :], ss.at[k], rs.at[k], tp_peer(k))

    def rows_wait(dst, ss, rs, k):
        there = dst.at[aligned(flip(tp, k), rows), :]
        rcopy(there, there, ss.at[k], rs.at[k], tp_peer(k)).wait_recv()

    def sb_copy(k):
        return rcopy(SB.at[tp], SB.at[tp], s_b.at[k], r_b.at[k], tp_peer(k))

    sends = []
    for k in (1, 2, 3):
        sends.append(sb_copy(k))
    for i in range(4):
        sends.append(wx_send(i))
    for i in range(4):
        sends.append(wc_send(i))
    for k in (2, 3, 1):
        sends.append(rows_copy(x_in, X, s_x, r_x, k))
    for i in (4, 5):
        sends.append(wx_send(i))
        sends.append(wc_send(i))
    for k in (2, 3, 1):
        sends.append(rows_copy(cot_in, COT, s_c, r_c, k))
    for copy in sends:
        copy.start()

    live_row = mask[pl.ds(tp, 1), :].astype(F32)
    LIVE[:, 0:8] = jnp.transpose(jnp.broadcast_to(live_row, (8, total)))
    ds_here = dataset[tp]
    off = jnp.zeros((1, X.shape[1]), F32)
    for c in range(dbias.shape[0]):
        off = off + jnp.where(ds_here == c, 1.0, 0.0) * dbias[c : c + 1, :].astype(F32)

    for copy in own:
        copy.wait()
    for k in (1, 2, 3):
        there = SB.at[flip(tp, k)]
        rcopy(there, there, s_b.at[k], r_b.at[k], tp_peer(k)).wait_recv()

    lane = lax.broadcasted_iota(jnp.int32, (half, LANES), 1)
    upper = lane >= HD
    one = jnp.ones((), BF)
    zero = jnp.zeros((), BF)

    def project(hh, first):
        rr = aligned(hh, half)
        ACT[rr, :] = (X[rr, :].astype(F32) + off).astype(BF)
        fill = jnp.where(LIVE[rr, 0:1] > 0.5, 0.0, NEG_FILL).astype(BF)
        fill = jnp.broadcast_to(fill, (half, LANES))

        def shard(k, carry):
            t = flip(tp, k)
            if first:
                @pl.when(k == 1)
                def _():
                    wc_wait(0)

                @pl.when(k == 2)
                def _():
                    wf_start(0)
                    wf_start(1)

                @pl.when(k == 3)
                def _():
                    wf_wait(0)

            qkv = nn(ACT[rr, :], WP[t])
            query = (qkv[:, :LANES] + SB[t, 0:1, :]).astype(BF) * BF(0.125)
            keys = qkv[:, LANES : 2 * LANES].astype(BF)
            vals = (qkv[:, 2 * LANES :] + SB[t, 1:2, :]).astype(BF)
            QA[2 * t, rr, :] = jnp.where(upper, jnp.where(lane == HD, one, zero), query)
            QA[2 * t + 1, rr, :] = jnp.where(upper, query, jnp.where(lane == 0, one, zero))
            KA[2 * t, rr, :] = jnp.where(upper, jnp.where(lane == HD, fill, zero), keys)
            KA[2 * t + 1, rr, :] = jnp.where(upper, keys, jnp.where(lane == 0, fill, zero))
            VA[2 * t, rr, :] = jnp.where(upper, -one, vals)
            VA[2 * t + 1, rr, :] = jnp.where(upper, vals, -one)
            return carry

        lax.fori_loop(0, 4, shard, 0)

    wq_start(0)
    wq_start(1)
    rows_wait(X, s_x, r_x, 1)
    project(x_id, True)
    rows_wait(X, s_x, r_x, 2)
    rows_wait(X, s_x, r_x, 3)
    project(1 - x_id, False)

    def attend(p, carry):
        @pl.when(p == 2)
        def _():
            wq_start(2)
            wq_start(3)

        for c in range(2):
            rr = pl.ds(c * half, half)
            outs = []
            for e in range(2):
                h = 2 * p + e
                scores = nt(QA[h, rr, :], KA[h])
                top = jnp.max(scores, axis=1, keepdims=True)
                weight = jnp.exp(scores - top).astype(BF)
                PR[h, rr, :] = weight
                outs.append(nn(weight, VA[h]))
            inv = -1.0 / jnp.where(upper, pltpu.roll(outs[1], HD, 1), pltpu.roll(outs[0], HD, 1))
            LINV[p, rr, :] = inv
            MIX[p, rr, :] = (jnp.where(upper, outs[1], outs[0]) * inv).astype(BF)
        return carry

    lax.fori_loop(0, 4, attend, 0)

    wc_wait(1)
    wf_wait(1)

    acc = nn(MIX[0], WO[0:LANES, :])
    for p in range(1, 4):
        acc = acc + nn(MIX[p], WO[p * LANES : (p + 1) * LANES, :])
    ACC[...] = acc

    step = total // 2
    gain0, gain1 = gain[0:1, :].astype(F32), gain[1:2, :].astype(F32)
    shift0, shift1 = shift[0:1, :].astype(F32), shift[1:2, :].astype(F32)
    ob0, ob1 = obias[0:1, :].astype(F32), obias[1:2, :].astype(F32)

    def norm_one(i, carry):
        rr = aligned(i, step)
        res = X[rr, :].astype(F32) + off + (ACC[rr, :] + ob0)
        cen = res - jnp.mean(res, axis=-1, keepdims=True)
        fac = lax.rsqrt(jnp.mean(cen * cen, axis=-1, keepdims=True) + EPSILON)
        nrm = cen * fac
        N1[rr, :] = nrm
        LIVE[rr, 1:2] = fac
        hid = nrm * gain0 + shift0
        HL[rr, :] = hid.astype(BF)
        ACC[rr, :] = hid + ob1
        return carry

    lax.fori_loop(0, 2, norm_one, 0)


    def ffn(k, carry):
        t = flip(tp, k)

        @pl.when(k == 1)
        def _():
            wc_wait(2)
            wc_wait(3)

        @pl.when(k == 2)
        def _():
            wf_start(2)
            wf_start(3)

        @pl.when(k == 3)
        def _():
            wf_wait(2)
            wf_wait(3)

        for c in range(2):
            rr = pl.ds(c * half, half)
            upper_bias = jnp.concatenate([SB[t, 2 + i : 3 + i, :] for i in range(4)], axis=1)
            u = nn(HL[rr, :], WU[t]) + upper_bias
            sq = u * u
            th = jnp.tanh(u * (GELU_C + (GELU_C * 0.044715) * sq))
            hp = 0.5 + 0.5 * th
            act = (u * hp).astype(BF)
            ACT2[t, rr, :] = act
            GP[t, rr, :] = (
                hp + (0.5 * u) * (1.0 - th * th) * (GELU_C + (3.0 * GELU_C * 0.044715) * sq)
            ).astype(BF)
            ACC[rr, :] += nn(act, WD[t])
        return carry

    lax.fori_loop(0, 4, ffn, 0)

    for k in (1, 2, 3):
        rows_wait(COT, s_c, r_c, k)

    SM[...] = jnp.zeros_like(SM)

    def norm_two(i, carry):
        rr = aligned(i, step)
        res = ACC[rr, :]
        cen = res - jnp.mean(res, axis=-1, keepdims=True)
        fac = lax.rsqrt(jnp.mean(cen * cen, axis=-1, keepdims=True) + EPSILON)
        nrm = cen * fac
        live = LIVE[rr, 0:1]
        gf = COT[rr, :].astype(F32) * live
        COT[rr, :] = ((nrm * gain1 + shift1) * live).astype(BF)
        gn = gf * gain1
        g2 = fac * (
            gn - jnp.mean(gn, axis=-1, keepdims=True) - nrm * jnp.mean(gn * nrm, axis=-1, keepdims=True)
        )
        ACC[rr, :] = g2
        G2L[rr, :] = g2.astype(BF)
        SM[5:6, :] += jnp.sum(gf * nrm, axis=0, keepdims=True)
        SM[7:8, :] += jnp.sum(gf, axis=0, keepdims=True)
        SM[9:10, :] += jnp.sum(g2, axis=0, keepdims=True)
        return carry

    lax.fori_loop(0, 2, norm_two, 0)

    def back_copy(buf, dst, ss, rs, k):
        return rcopy(buf.at[aligned(flip(tp, k), rows), :], dst.at[tp], ss.at[k], rs.at[k], tp_peer(k))

    def back_wait(buf, dst, ss, rs, k):
        there = dst.at[flip(tp, k)]
        rcopy(buf.at[aligned(tp, rows), :], there, ss.at[k], rs.at[k], tp_peer(k)).wait_recv()

    outs_sent = [back_copy(COT, out_rows, s_out, r_out, k) for k in (2, 3, 1)]
    outs_sent[0].start()
    outs_sent[2].start()
    out_local = pltpu.make_async_copy(COT.at[aligned(tp, rows), :], out_rows.at[tp], s_loc.at[0])
    out_local.start()

    pieces = ((0, 0, width), (1, 0, width)) + tuple((2, g * LANES, LANES) for g in (3, 2, 1, 0))

    def gref(i, t):
        m, r0, n = pieces[i]
        return WU.at[t, pl.ds(r0, n), :] if m == 2 else G.at[m, t]

    def gchunk(i, t, q):
        m, r0, n = pieces[i]
        at = pl.ds(pl.multiple_of(r0 + q * (n // quad), 16), n // quad)
        return WU.at[t, at, :] if m == 2 else G.at[m, t, at, :]

    def rxchunk(i, q):
        m, r0, n = pieces[i]
        return RX.at[m, pl.ds(pl.multiple_of(r0 + q * (n // quad), 16), n // quad), :]

    def span(i):
        return pl.ds(pieces[i][1], pieces[i][2])

    def qspan(i):
        return pl.ds(pieces[i][1] // quad, pieces[i][2] // quad)

    def core_send(i, j):
        there = RC.at[pieces[i][0], j, span(i), :]
        return rcopy(gref(i, flip(tp, 1 if j == 0 else 3)), there, s_rc.at[i, j], r_rc.at[i, j], tp_peer(1))

    def core_add(i, j):
        there = RC.at[pieces[i][0], j, span(i), :]
        rcopy(there, there, s_rc.at[i, j], r_rc.at[i, j], tp_peer(1)).wait_recv()
        ref = gref(i, flip(tp, 2) if j == 1 else tp)
        ref[...] = (ref[...].astype(F32) + there[...].astype(F32)).astype(BF)

    def x_send(i):
        if i == 1:
            src, dst = gchunk(i, flip(tp, 2), q_id), rxchunk(i, q_id)
        else:
            src, dst = gref(i, flip(tp, 2)), RX.at[pieces[i][0], span(i), :]
        return rcopy(src, dst, s_rx.at[i], r_rx.at[i], tp_peer(2))

    def quad_send(i, j, other=False):
        if other:
            return rcopy(gchunk(i, flip(tp, 2), quad_at(j)), RB.at[j - 1], s_rb.at[j - 1], r_rb.at[j - 1], quad_peer(j))
        there = RQ.at[pieces[i][0], j - 1, qspan(i), :]
        return rcopy(gchunk(i, tp, quad_at(j)), there, s_rq.at[i, j - 1], r_rq.at[i, j - 1], quad_peer(j))

    def quad_start(i, other=False):
        for j in range(1, quad):
            quad_send(i, j, other).start()

    def rest_send(i, j):
        here = RE.at[pieces[i][0], r_id, qspan(i), :]
        return rcopy(here, here, s_re.at[i, j - 1], r_re.at[i, j - 1], rest_peer(j))

    def ag_send(i, j):
        here = rxchunk(i, q_id)
        return rcopy(here, here, s_ag.at[i, j - 1], r_ag.at[i, j - 1], quad_peer(j))

    def reduce_x(i):
        core_add(i, 1)
        x_send(i).start()

    def reduce_quad(i):
        core_add(i, 0)
        x_send(i).wait_recv()
        ref = gref(i, tp)
        ref[...] = (ref[...].astype(F32) + RX[pieces[i][0], span(i), :].astype(F32)).astype(BF)
        quad_start(i)

    def reduce_other(i):
        for j in range(1, quad):
            quad_send(i, j, True).wait_recv()
        ref = gchunk(i, flip(tp, 2), q_id)
        acc_q = ref[...].astype(F32)
        for j in range(quad - 1):
            acc_q = acc_q + RB[j].astype(F32)
        ref[...] = acc_q.astype(BF)
        x_send(i).start()

    def reduce_rest(i):
        m = pieces[i][0]
        for j in range(1, quad):
            quad_send(i, j).wait_recv()
        acc_q = gchunk(i, tp, q_id)[...].astype(F32)
        for j in range(quad - 1):
            acc_q = acc_q + RQ[m, j, qspan(i), :].astype(F32)
        if i == 1:
            x_send(i).wait_recv()
            acc_q = acc_q + rxchunk(i, q_id)[...].astype(F32)
        RE[m, r_id, qspan(i), :] = acc_q.astype(BF)
        for j in range(1, rest_n):
            rest_send(i, j).start()

    def reduce_gather(i):
        m = pieces[i][0]
        for j in range(1, rest_n):
            there = RE.at[m, lax.rem(r_id + rest_n - j, rest_n), qspan(i), :]
            rcopy(there, there, s_re.at[i, j - 1], r_re.at[i, j - 1], rest_peer(j)).wait_recv()
        acc_r = RE[m, 0, qspan(i), :].astype(F32)
        for j in range(1, rest_n):
            acc_r = acc_r + RE[m, j, qspan(i), :].astype(F32)
        here = rxchunk(i, q_id)
        here[...] = acc_r.astype(BF)
        for j in range(1, quad):
            ag_send(i, j).start()

    def reduce_done(i):
        for j in range(1, quad):
            there = rxchunk(i, quad_at(-j))
            rcopy(there, there, s_ag.at[i, j - 1], r_ag.at[i, j - 1], quad_peer(j)).wait_recv()


    def ffn_back(k, carry):
        t = flip(tp, 3 - k)
        d_act = nt(G2L[...], WD[t])
        g_pre = d_act * GP[t].astype(F32)
        SM[pl.ds(10 + t, 1), :] = jnp.sum(g_pre, axis=0, keepdims=True)
        low = g_pre.astype(BF)
        GP[t] = low
        G[0, t] = tn(ACT2[t], G2L[...]).astype(BF)
        G[1, t] = tn(HL[...], low).astype(BF)
        ACC[...] += nt(low, WU[t])

        @pl.when(k == 0)
        def _():
            core_send(0, 1).start()
            core_send(1, 1).start()

        @pl.when(k == 1)
        def _():
            reduce_x(0)
            core_add(1, 1)
            quad_start(1, True)

        @pl.when(k == 2)
        def _():
            core_send(0, 0).start()
            core_send(1, 0).start()

        @pl.when(k == 3)
        def _():
            core_add(1, 0)
            quad_start(1)

        return carry

    lax.fori_loop(0, 4, ffn_back, 0)

    def norm_one_back(i, carry):
        rr = aligned(i, step)
        gh = ACC[rr, :]
        nrm = N1[rr, :]
        gn = gh * gain0
        g1 = LIVE[rr, 1:2] * (
            gn - jnp.mean(gn, axis=-1, keepdims=True) - nrm * jnp.mean(gn * nrm, axis=-1, keepdims=True)
        )
        ACC[rr, :] = g1
        G2L[rr, :] = g1.astype(BF)
        SM[4:5, :] += jnp.sum(gh * nrm, axis=0, keepdims=True)
        SM[6:7, :] += jnp.sum(gh, axis=0, keepdims=True)
        SM[8:9, :] += jnp.sum(g1, axis=0, keepdims=True)
        return carry

    lax.fori_loop(0, 2, norm_one_back, 0)

    def back_prep(p, carry):
        gm = nt(G2L[...], WO[aligned(p, LANES), :])
        WU[p, pl.ds(3 * LANES, LANES), :] = tn(MIX[p], G2L[...]).astype(BF)
        lane_f = lax.broadcasted_iota(jnp.int32, (total, LANES), 1)
        up_f = lane_f >= HD
        gs = gm * LINV[p]
        prod = gs * MIX[p].astype(F32)
        low = gs.astype(BF)
        for e in range(2):
            mine = up_f if e == 1 else jnp.logical_not(up_f)
            delta = jnp.sum(jnp.where(mine, prod, 0.0), axis=-1, keepdims=True)
            hi = delta.astype(BF)
            lo = (delta - hi.astype(F32)).astype(BF)
            base = HD * (1 - e)
            side = jnp.where(lane_f == base, hi, jnp.where(lane_f == base + 1, lo, zero))
            GP[p, :, pl.ds(e * LANES, LANES)] = jnp.where(mine, low, side)
        return carry

    wf_send(2).wait_send()
    for j in range(1, quad):
        wq_send(2, j).wait_send()
    lax.fori_loop(0, 4, back_prep, 0)
    core_send(2, 1).start()
    core_send(2, 0).start()
    reduce_other(1)

    ones = jnp.ones((8, total), BF)
    lane_f = lax.broadcasted_iota(jnp.int32, (total, LANES), 1)
    up_f = lane_f >= HD

    def attend_back(k, carry):
        p = flip(tp, 3 - k)

        def at(where, what):
            @pl.when(k == where)
            def _():
                for fun in what:
                    fun()

        def join(cols, group):
            low = jnp.where(up_f, cols[1], cols[0]).astype(BF)
            ACT2[p, :, group * LANES : (group + 1) * LANES] = low
            WU[p, group * LANES : (group + 1) * LANES, :] = tn(low, ACT[...]).astype(BF)
            SD[p, 0:1, group * LANES : (group + 1) * LANES] = jnp.sum(low.astype(F32), axis=0, keepdims=True)

        def join_t(parts, group):
            low_t = jnp.concatenate([parts[0][:HD], parts[1][HD:]], axis=0).astype(BF)
            WU[p, group * LANES : (group + 1) * LANES, :] = nn(low_t, ACT[...]).astype(BF)
            low = jnp.transpose(low_t)
            ACT2[p, :, group * LANES : (group + 1) * LANES] = low
            SD[p, 0:1, group * LANES : (group + 1) * LANES] = jnp.sum(low.astype(F32), axis=0, keepdims=True)

        def hooks(step):
            for where, todo in enumerate(plan[step]):
                if todo:
                    at(where, todo)

        cols = []
        for e in range(2):
            cols.append(tn(GP[p, :, pl.ds(e * LANES, LANES)], PR[2 * p + e]))
        join_t(cols, 2)
        hooks(0)
        cols = []
        for e in range(2):
            h = 2 * p + e
            for c in range(2):
                rr = pl.ds(c * half, half)
                d_p = nt(GP[p, rr, pl.ds(e * LANES, LANES)], VA[h])
                PR[h, rr, :] = (PR[h, rr, :].astype(F32) * d_p).astype(BF)
            cols.append(tn(QA[h], PR[h]))
        join_t(cols, 1)
        hooks(1)
        cols = []
        for e in range(2):
            h = 2 * p + e
            cols.append(nn(PR[h], KA[h]) * 0.125)
        join(cols, 0)
        hooks(2)
        return carry

    def act(fun, *args):
        return lambda: fun(*args)

    def send(fun, *args):
        return lambda: fun(*args).start()

    plan = (
        (
            (send(core_send, 3, 1), act(reduce_x, 2)),
            (act(reduce_x, 3),),
            (send(core_send, 3, 0), act(reduce_quad, 2)),
            (act(reduce_quad, 3), act(reduce_rest, 2)),
        ),
        (
            (send(core_send, 4, 1),),
            (act(reduce_x, 4),),
            (send(core_send, 4, 0),),
            (act(reduce_quad, 4),),
        ),
        (
            (send(core_send, 5, 1), act(reduce_quad, 0)),
            (act(reduce_x, 5), outs_sent[1].start, act(reduce_rest, 1)),
            (send(core_send, 5, 0), act(reduce_rest, 0)),
            (act(reduce_quad, 5),),
        ),
    )
    lax.fori_loop(0, 4, attend_back, 0)

    base_sum = SM[8:9, :]
    for p in range(4):
        sums = jnp.broadcast_to(SD[p, 0:1, :], (8, 3 * LANES))
        SM[14:15, p * LANES : (p + 1) * LANES] = sums[0:1, 0:LANES]
        SM[15:16, p * LANES : (p + 1) * LANES] = sums[0:1, 2 * LANES : 3 * LANES]
        hi = sums.astype(BF)
        rem = sums - hi.astype(F32)
        mid = rem.astype(BF)
        low = (rem - mid.astype(F32)).astype(BF)
        for term in (hi, mid, low):
            base_sum = base_sum + nt(term, WP[p])[0:1, :]
    for c in range(dbias.shape[0]):
        SM[c : c + 1, :] = jnp.where(ds_here == c, 1.0, 0.0) * base_sum

    stages = (
        (SMT, tp, 4, 0, tp_peer, lambda j: flip(tp, j)),
        (SMQ, q_id, quad, 4, quad_peer, lambda j: quad_at(-j)),
        (SMR, r_id, rest_n, 4 + quad, rest_peer, lambda j: lax.rem(r_id + rest_n - j, rest_n)),
    )

    def sm_send(stage, j):
        slots, me, count, sem0, peer_of, from_of = stages[stage]
        return rcopy(slots.at[me], slots.at[me], s_sm.at[sem0 + j], r_sm.at[sem0 + j], peer_of(j))

    def sm_start(stage, value):
        slots, me, count, sem0, peer_of, from_of = stages[stage]
        slots[me] = value
        for j in range(1, count):
            sm_send(stage, j).start()

    def sm_sum(stage):
        slots, me, count, sem0, peer_of, from_of = stages[stage]
        for j in range(1, count):
            there = slots.at[from_of(j)]
            rcopy(there, there, s_sm.at[sem0 + j], r_sm.at[sem0 + j], peer_of(j)).wait_recv()
        value = slots[0]
        for j in range(1, count):
            value = value + slots[j]
        return value

    sm_start(0, SM[...])
    reduce_gather(1)
    reduce_gather(2)

    def input_grad(k, carry):
        b = flip(tp, 3 - k)
        rr = aligned(b, rows)
        grad = ACC[rr, :]
        for p in range(4):
            grad = grad + nt(ACT2[p, rr, 0 : 3 * LANES], WP[p])
        X[rr, :] = grad.astype(BF)

        @pl.when(k < 3)
        def _():
            kk = 3 - k
            rcopy(X.at[rr, :], ig_rows.at[tp], s_ig.at[kk], r_ig.at[kk], (dp, b)).start()

        return carry

    lax.fori_loop(0, 4, input_grad, 0)
    ig_local = pltpu.make_async_copy(X.at[aligned(tp, rows), :], ig_rows.at[tp], s_loc.at[1])
    ig_local.start()

    sm_start(1, sm_sum(0))
    reduce_rest(3)
    reduce_rest(4)
    reduce_rest(5)
    reduce_gather(0)
    sm_start(2, sm_sum(1))
    reduce_gather(3)
    reduce_gather(4)
    reduce_gather(5)
    results = []
    for m, done in enumerate(((0,), (1,), (2, 3, 4, 5))):
        for i in done:
            reduce_done(i)
        results.append(pltpu.make_async_copy(RX.at[m], g_sum.at[m], s_res.at[m]))
        results[-1].start()

    g_small[...] = sm_sum(2)
    for k in (1, 2, 3):
        back_wait(COT, out_rows, s_out, r_out, k)
        back_wait(X, ig_rows, s_ig, r_ig, k)
        back_copy(X, ig_rows, s_ig, r_ig, k).wait_send()
    ig_local.wait()
    out_local.wait()
    for result in results:
        result.wait()
    for copy in sends + outs_sent:
        copy.wait_send()
    for stage in range(3):
        for j in range(1, stages[stage][2]):
            sm_send(stage, j).wait_send()
    for g in (0, 1, 3):
        wf_send(g).wait_send()
        for j in range(1, quad):
            wq_send(g, j).wait_send()
    for i in range(6):
        core_send(i, 0).wait_send()
        core_send(i, 1).wait_send()
        x_send(i).wait_send()
        for j in range(1, quad):
            quad_send(i, j).wait_send()
            ag_send(i, j).wait_send()
            if i == 1:
                quad_send(i, j, True).wait_send()
        for j in range(1, rest_n):
            rest_send(i, j).wait_send()


def finish(
    raw_out, raw_ig, g_sum, g_small,
    out_rows, ig_rows, g_qkv, g_out, g_up, g_down, g_dbias, g_gain, g_shift, g_obias, g_upb, g_qvb,
):
    i = pl.program_id(0)
    tp = lax.axis_index("tp")
    out_rows[...] = raw_out[...]
    ig_rows[...] = raw_ig[...]
    g_down[...] = g_sum[0].astype(F32)
    g_up[...] = g_sum[1].astype(F32)

    @pl.when(i < 3)
    def _():
        g_qkv[0] = jnp.transpose(g_sum[2].astype(F32))

    @pl.when(i == 3)
    def _():
        g_out[...] = g_sum[2].astype(F32)

    @pl.when(i == 0)
    def _():
        g_dbias[...] = g_small[0:4, :]
        g_gain[...] = g_small[4:6, :]
        g_shift[...] = g_small[6:8, :]
        g_obias[...] = g_small[8:10, :]
        g_upb[...] = g_small[pl.ds(10 + tp, 1), :]
        g_qvb[...] = g_small[14:16, aligned(tp, LANES)]


def shards(dp_n, *args):
    (inputs, dataset, variate_mask, dataset_bias, w_qkv, qv_bias, w_out, out_bias, w_up, up_bias, w_down,
     norm_gain, norm_shift, cotangent) = args
    win, rows, width = inputs.shape
    total = variate_mask.shape[1]
    quad = 4 if dp_n <= 16 else 8
    rest_n = dp_n // quad
    ffs = w_up.shape[1]
    assert win == 4 and total == 4 * rows and width == 512 and ffs == 512 and w_out.shape[0] == LANES
    any_spec = pl.BlockSpec(memory_space=pl.ANY)
    vmem = pl.BlockSpec(memory_space=pltpu.VMEM)
    smem = pl.BlockSpec(memory_space=pltpu.SMEM)
    dma = pltpu.SemaphoreType.DMA
    V = pltpu.VMEM
    scratch = [
        V((total, width), BF),
        V((total, width), BF),
        V((4, width, 3 * LANES), BF),
        V((width, width), BF),
        V((4, width, ffs), BF),
        V((4, ffs, width), BF),
        V((4, 8, LANES), F32),
        V((total, width), BF),
        V((8, total, LANES), BF),
        V((8, total, LANES), BF),
        V((8, total, LANES), BF),
        V((8, total, total), BF),
        V((4, total, LANES), BF),
        V((4, total, LANES), F32),
        V((total, width), F32),
        V((total, width), BF),
        V((4, total, ffs), BF),
        V((4, total, ffs), BF),
        V((total, width), F32),
        V((total, width), BF),
        V((total, LANES), F32),
        V((2, 4, width, ffs), BF),
        V((3, 2, width, ffs), BF),
        V((3, width, ffs), BF),
        V((3, quad - 1, width // quad, ffs), BF),
        V((quad - 1, width // quad, ffs), BF),
        V((3, rest_n, width // quad, ffs), BF),
        V((4, 8, 3 * LANES), F32),
        V((16, width), F32),
        V((4, 16, width), F32),
        V((quad, 16, width), F32),
        V((rest_n, 16, width), F32),
        dma((8,)),
        dma((4,)), dma((4,)),
        dma((4,)), dma((4,)),
        dma((6,)), dma((6,)),
        dma((4, quad - 1)), dma((4, quad - 1)),
        dma((4,)), dma((4,)),
        dma((6,)), dma((6,)),
        dma((4,)), dma((4,)),
        dma((4,)), dma((4,)),
        dma((4,)), dma((4,)),
        dma((2,)),
        dma((6, 2)), dma((6, 2)),
        dma((6,)), dma((6,)),
        dma((6, quad - 1)), dma((6, quad - 1)),
        dma((quad - 1,)), dma((quad - 1,)),
        dma((6, max(rest_n - 1, 1))), dma((6, max(rest_n - 1, 1))),
        dma((6, quad - 1)), dma((6, quad - 1)),
        dma((4 + quad + rest_n,)), dma((4 + quad + rest_n,)),
        dma((3,)),
    ]
    sds = jax.ShapeDtypeStruct
    outs = pl.pallas_call(
        functools.partial(kernel, quad, rest_n),
        out_shape=(
            sds((win, rows, width), BF),
            sds((win, rows, width), BF),
            sds((3, width, ffs), BF),
            sds((16, width), F32),
        ),
        in_specs=[any_spec, any_spec, smem, vmem, vmem, any_spec, vmem, any_spec, vmem, any_spec, vmem, any_spec, vmem, vmem],
        out_specs=(any_spec,) * 3 + (vmem,),
        scratch_shapes=scratch,
        compiler_params=pltpu.CompilerParams(
            collective_id=0, has_side_effects=True, vmem_limit_bytes=65000000
        ),
        cost_estimate=pl.CostEstimate(flops=30 * 10**9, bytes_accessed=20 * 10**6, transcendentals=10**7),
        name="encoder_layer",
    )(inputs, cotangent, dataset, variate_mask, dataset_bias, w_qkv, qv_bias, w_out, out_bias, w_up,
      up_bias.reshape(4, LANES), w_down, norm_gain, norm_shift)
    raw_out, raw_ig, g_sum, g_small = outs
    res = pl.pallas_call(
        finish,
        out_shape=(
            sds((win, rows, width), BF),
            sds((win, rows, width), BF),
            sds((3, width, LANES), F32),
            sds((LANES, width), F32),
            sds((width, ffs), F32),
            sds((ffs, width), F32),
            sds((4, width), F32),
            sds((2, width), F32),
            sds((2, width), F32),
            sds((2, width), F32),
            sds((1, width), F32),
            sds((2, LANES), F32),
        ),
        grid=(4,),
        in_specs=[
            pl.BlockSpec((1, rows, width), lambda i: (i, 0, 0)),
            pl.BlockSpec((1, rows, width), lambda i: (i, 0, 0)),
            pl.BlockSpec((3, LANES, ffs), lambda i: (0, i, 0)),
            pl.BlockSpec((16, width), lambda i: (0, 0)),
        ],
        out_specs=(
            pl.BlockSpec((1, rows, width), lambda i: (i, 0, 0)),
            pl.BlockSpec((1, rows, width), lambda i: (i, 0, 0)),
            pl.BlockSpec((1, width, LANES), lambda i: (jnp.minimum(i, 2), 0, 0)),
            pl.BlockSpec((LANES, width), lambda i: (0, 0)),
            pl.BlockSpec((LANES, ffs), lambda i: (i, 0)),
            pl.BlockSpec((LANES, width), lambda i: (i, 0)),
            pl.BlockSpec((4, width), lambda i: (0, 0)),
            pl.BlockSpec((2, width), lambda i: (0, 0)),
            pl.BlockSpec((2, width), lambda i: (0, 0)),
            pl.BlockSpec((2, width), lambda i: (0, 0)),
            pl.BlockSpec((1, width), lambda i: (0, 0)),
            pl.BlockSpec((2, LANES), lambda i: (0, 0)),
        ),
        name="write_results",
    )(raw_out, raw_ig, g_sum, g_small)
    (rows_out, rows_ig, g_qkv, g_out, g_up, g_down, g_dbias, g_gain, g_shift, g_obias, g_upb, g_qvb) = res
    return (
        rows_out, rows_ig, g_dbias, g_qkv, g_qvb, g_out, g_obias, g_up, g_upb.reshape(-1), g_down, g_gain, g_shift,
    )


def solution(mesh):
    in_specs = (
        P("dp", "tp", None), P("dp"), P("dp", None), P(), P(None, None, "tp"), P(None, "tp"), P("tp", None), P(),
        P(None, "tp"), P("tp"), P("tp", None), P(), P(), P("dp", "tp", None),
    )
    out_specs = (
        P("dp", "tp", None), P("dp", "tp", None), P(), P(None, None, "tp"), P(None, "tp"), P("tp", None), P(),
        P(None, "tp"), P("tp"), P("tp", None), P(), P(),
    )
    body = functools.partial(shards, mesh.shape["dp"])
    return jax.shard_map(body, mesh=mesh, in_specs=in_specs, out_specs=out_specs, check_vma=False)
```
